256 devices in a mesh: slab: 32 (over z_lo, y, core), tm: 8 (over x, z_hi).
Axes of the slice: x: 4, y: 4, z: 8 (z_hi: 2, z_lo: 4; z = z_hi * 4 + z_lo), core: 2. Of those that a mesh axis runs over, the one named last changes fastest.
Arguments:
- recording: bfloat16 [512, 65536], P('tm', 'slab'), may hold values from -6 to 6
- footprints: bfloat16 [2176, 8192], P(None, 'slab'), may hold values from -0.125 to 0.125
- traces: float32 [512, 8192], P('tm', 'slab'), may hold values from 0 to 2
- live_count: int32 [32], replicated, may hold values from 1 to 256, 6144 in all
Outputs:
- new_traces: float32 [512, 8192], P('tm', 'slab')
- new_footprints: bfloat16 [2176, 8192], P('tm', 'slab')
The draws below stay inside these ranges and needn't reach their ends.
Inputs may be any that keep to these rules, and one draw needn't show every extreme that they name: Slots 0 .. live_count[s] - 1 of slab s are live; some slab has all 256 live.
All inputs are finite; a program needn't handle non-finite values.
Results may differ from the reference program's by a relative error of at most 0.0034.
Values may be sent and summed in bfloat16 or wider, within the bound.
A program may use at most 64 MiB of HBM per device.

```python
import math
import jax
import jax.numpy as jnp
import numpy as np
from jax import lax

FRAMES = 512
GROUP = 128
GROUPS_DEV = 2
VOX_DEV = 2048
RIM = 128
K_DEV = 256
SLABS = 32
NEURONS = 8192
VOXELS = 65536
N_SLAB = 32


def level_of(rng, dims, split, least, high):
    def one(axis_at, blocks):
        draws = jax.random.uniform(jax.random.fold_in(jax.random.fold_in(rng, 6), axis_at), (blocks,), jnp.float32, least / len(split), high / len(split))
        return jnp.repeat(jnp.exp(draws), dims[axis_at] // blocks).reshape((-1,) + (1,) * (len(dims) - axis_at - 1))

    gain = one(*split[0])
    for cut in split[1:]:
        gain = gain * one(*cut)
    return gain


def split_up(number_of, total, bound, lean):
    weights = [(1 << 20) // math.isqrt(rank ** lean) + 1 for rank in range(2, number_of + 1)]
    rest, holding = total - bound - (number_of - 1), [1] * (number_of - 1)
    while rest > 0:
        free = [i for i in range(number_of - 1) if holding[i] < bound]
        pool, budget = sum([weights[i] for i in free]), rest
        for i in free:
            more = min(bound - holding[i], max(1, budget * weights[i] // pool), rest)
            holding[i] = holding[i] + more
            rest = rest - more
    return np.array([bound] + holding)


def ragged_sizes(rng, amount, total, limit, lean):
    if amount == 2:
        one = jax.random.randint(rng, (), max(1, total - limit), min(limit, total - 1) + 1)
        return jnp.stack([one, total - one])
    tallies = jnp.asarray(split_up(amount, total, limit, lean), jnp.int32)
    twos = (amount - 1) // 2
    giver, sink = tallies[1:1 + 2 * twos:2], tallies[2:2 + 2 * twos:2]
    room = jnp.minimum(giver - 1, limit - sink)
    passed = jax.random.randint(jax.random.fold_in(rng, 1), (twos,), 0, 1 << 20) % (room + 1)
    tallies = tallies.at[1:1 + 2 * twos:2].set(giver - passed).at[2:2 + 2 * twos:2].set(sink + passed)
    return tallies[jax.random.permutation(jax.random.fold_in(rng, 2), amount)]


def gaussian(stream_key, dims, width, bound, split=(), kind=jnp.bfloat16):
    entries = width * jax.random.normal(stream_key, dims, jnp.float32)
    if split:
        entries = entries * level_of(stream_key, dims, split, -0.22, 0.18)
    return jnp.clip(entries, -bound, bound).astype(kind)


def setup_inputs(seed: int = 0) -> dict:
    arg_keys = jax.random.split(jax.random.key(seed), 5)
    return {
        "recording": gaussian(arg_keys[0], (FRAMES, VOXELS), 1.0, 6.0, ((0, 8), (1, 32))),
        "footprints": gaussian(arg_keys[1], (VOX_DEV + RIM, NEURONS), (VOX_DEV + RIM) ** -0.5, 0.125, ((1, 32),)),
        "traces": jnp.clip(2.0 * jax.random.uniform(arg_keys[2], (FRAMES, NEURONS), jnp.float32) ** level_of(arg_keys[2], (FRAMES, NEURONS), ((0, 8), (1, 32)), -0.2, 0.2), 0.0, 2.0),
        "live_count": ragged_sizes(arg_keys[3], SLABS, SLABS * K_DEV * 3 // 4, K_DEV, 2).astype(jnp.int32),
    }


def contract_first(left, right):
    return lax.dot_general(left, right, (((0,), (0,)), ((), ())), preferred_element_type=jnp.float32)


def shifted_pair(stacked):
    empty = jnp.zeros_like(stacked[:1])
    return jnp.concatenate([empty, stacked[:-1]], 0), jnp.concatenate([stacked[1:], empty], 0)


def reference(recording, footprints, traces, live_count):
    extended = VOX_DEV + RIM
    slots = jnp.arange(K_DEV, dtype=jnp.int32)
    living = slots[None, :] < live_count[:, None]
    row_ids = jnp.arange(extended, dtype=jnp.int32)
    slab_ids = jnp.arange(N_SLAB, dtype=jnp.int32)
    row_keep = (row_ids[None, :] < VOX_DEV) | (slab_ids[:, None] < N_SLAB - 1)
    stacked = footprints.reshape(extended, N_SLAB, K_DEV).transpose(1, 0, 2)
    stacked = jnp.where(living[:, None, :] & row_keep[:, :, None], stacked, jnp.zeros_like(stacked))
    start_tr = traces.reshape(FRAMES, N_SLAB, K_DEV).transpose(1, 0, 2)
    start_tr = jnp.where(living[:, None, :], start_tr, jnp.zeros_like(start_tr))
    movie_slabs = recording.reshape(FRAMES, N_SLAB, VOX_DEV).transpose(1, 0, 2)
    movie_prev, movie_next = shifted_pair(movie_slabs)
    y_ext = jnp.concatenate([movie_slabs, movie_next[:, :, :RIM]], 2)
    rim_prev, unused_rim = shifted_pair(stacked[:, VOX_DEV:])
    unused_edge, edge_next = shifted_pair(stacked[:, :RIM])
    traces_prev, traces_next = shifted_pair(start_tr)

    def trace_slab(items):
        masked_foot, movie_ext, prev_rim, next_edge, current, prev_c, next_c = items
        drive = jnp.dot(movie_ext, masked_foot, preferred_element_type=jnp.float32)
        gram_own = contract_first(masked_foot, masked_foot)
        gram_prev = contract_first(masked_foot[:RIM], prev_rim)
        gram_next = contract_first(masked_foot[VOX_DEV:], next_edge)
        diag_own = jnp.diagonal(gram_own) + 1e-6
        outside = jnp.dot(prev_c, gram_prev.T, precision=lax.Precision.HIGHEST) + jnp.dot(next_c, gram_next.T, precision=lax.Precision.HIGHEST)
        for group_id in range(GROUPS_DEV):
            offset = group_id * GROUP
            coupled = jnp.dot(current, gram_own[:, offset:offset + GROUP], precision=lax.Precision.HIGHEST) + outside[:, offset:offset + GROUP]
            updated = jnp.maximum(current[:, offset:offset + GROUP] + (drive[:, offset:offset + GROUP] - coupled) / diag_own[offset:offset + GROUP], 0.0)
            current = current.at[:, offset:offset + GROUP].set(updated)
        return current

    new_tr = lax.map(trace_slab, (stacked, y_ext, rim_prev, edge_next, start_tr, traces_prev, traces_next))
    rounded = new_tr.astype(jnp.bfloat16)
    rounded_prev, rounded_next = shifted_pair(rounded)

    def foot_slab(items):
        masked_foot, movie_ext, prev_rim, next_edge, own_c, prev_c, next_c = items
        proj_rows = contract_first(movie_ext, own_c)
        q_own = contract_first(own_c, own_c)
        q_prev = contract_first(prev_c, own_c)
        q_next = contract_first(next_c, own_c)
        divisor = jnp.maximum(jnp.diagonal(q_own), 1.0)
        foot_f = masked_foot.astype(jnp.float32)
        coupling = jnp.dot(foot_f, q_own, precision=lax.Precision.HIGHEST)
        coupling = coupling.at[:RIM].add(jnp.dot(prev_rim.astype(jnp.float32), q_prev, precision=lax.Precision.HIGHEST))
        coupling = coupling.at[VOX_DEV:].add(jnp.dot(next_edge.astype(jnp.float32), q_next, precision=lax.Precision.HIGHEST))
        return jnp.maximum(foot_f + (proj_rows - coupling) / divisor, 0.0).astype(jnp.bfloat16)

    new_foot = lax.map(foot_slab, (stacked, y_ext, rim_prev, edge_next, rounded, rounded_prev, rounded_next))
    out_traces = new_tr.transpose(1, 0, 2).reshape(FRAMES, NEURONS)
    out_foot = new_foot.transpose(1, 0, 2).reshape(extended, NEURONS)
    return out_traces, out_foot
```

```python
import functools

import jax
import jax.numpy as jnp
from jax import lax
from jax.experimental import pallas as pl
from jax.experimental.pallas import tpu as pltpu
from jax.sharding import PartitionSpec as P

MESH = pl.DeviceIdType.MESH
F32 = jnp.float32
BF16 = jnp.bfloat16
GROUP = 128


def dot(a, b, ca=1, cb=0, precision=None):
    return lax.dot_general(
        a, b, (((ca,), (cb,)), ((), ())), preferred_element_type=F32, precision=precision
    )


def halves(x):
    high = x.astype(BF16)
    return high, (x - high.astype(F32)).astype(BF16)


def remote(src, dst, sems, index, **device):
    return pltpu.make_async_remote_copy(
        src_ref=src,
        dst_ref=dst,
        send_sem=sems[0].at[index[0]],
        recv_sem=sems[1].at[index[1]],
        device_id=device,
        device_id_type=MESH,
    )


def exchange_kernel(
    dims,
    live_ref, y_hbm, a_hbm, c_hbm,
    tr_out, b_all, yt_out, side_out, share_out,
    yv, av, cv, y_send, y_recv, rim_in, head_out, tail_out, head_in, tail_in,
    side_head, side_tail,
    load_sem, y_ss, y_rs, b_ss, b_rs, h_ss, h_rs, s_ss, s_rs,
):
    slabs, parts, frames, voxels, rows, neurons = dims
    rim = rows - voxels
    share = rows // parts
    wide = share // 128 * 128
    rest = share - wide
    s = lax.axis_index("slab")
    t = lax.axis_index("tm")
    has_next = s < slabs - 1
    has_prev = s > 0
    first, last = t == 0, t == parts - 1

    loads = [
        pltpu.make_async_copy(c_hbm, cv, load_sem.at[0]),
        pltpu.make_async_copy(a_hbm.at[:rim], av.at[:rim], load_sem.at[1]),
        pltpu.make_async_copy(a_hbm.at[voxels:], av.at[voxels:], load_sem.at[2]),
        pltpu.make_async_copy(y_hbm, yv, load_sem.at[3]),
        pltpu.make_async_copy(a_hbm.at[rim:voxels], av.at[rim:voxels], load_sem.at[4]),
    ]
    for load in loads:
        load.start()

    barrier = pltpu.get_barrier_semaphore()

    def greet(**device):
        pl.semaphore_signal(barrier, inc=1, device_id=device, device_id_type=MESH)

    for i in range(1, parts):
        greet(tm=lax.rem(t + i, parts))

    @pl.when(has_next)
    def _():
        greet(slab=s + 1)

    @pl.when(has_prev)
    def _():
        greet(slab=s - 1)

    @pl.when(first & has_prev)
    def _():
        for i in range(1, parts):
            greet(slab=s - 1, tm=t + i)

    @pl.when(last & has_next)
    def _():
        for i in range(1, parts):
            greet(slab=s + 1, tm=t - i)

    one = jnp.int32(1)
    zero = jnp.int32(0)
    pl.semaphore_wait(
        barrier,
        parts - 1
        + jnp.where(has_next, jnp.where(first, one, one + 1), zero)
        + jnp.where(has_prev, jnp.where(last, one, one + 1), zero),
    )

    rim_copy = remote(y_hbm.at[:, :rim], rim_in, (h_ss, h_rs), (0, 0), slab=s - 1)
    head_copy = remote(head_out, head_in, (h_ss, h_rs), (1, 1), slab=s - 1)
    tail_copy = remote(tail_out, tail_in, (h_ss, h_rs), (2, 2), slab=s + 1)

    @pl.when(has_prev)
    def _():
        rim_copy.start()

    live = lax.broadcasted_iota(jnp.int32, (1, neurons), 1) < live_ref[s]
    for load in loads[:3]:
        load.wait()
    keep_tail = jnp.where(has_next, 1.0, 0.0).astype(F32)
    start = jnp.where(live, cv[...], 0.0)
    c_high, c_low = halves(start)
    head = av[:rim]
    tail = (av[voxels:].astype(F32) * keep_tail).astype(BF16)
    av[voxels:] = tail
    head_out[...] = dot(c_high, head, 1, 1) + dot(c_low, head, 1, 1)
    tail_out[...] = dot(c_high, tail, 1, 1) + dot(c_low, tail, 1, 1)

    @pl.when(has_prev)
    def _():
        head_copy.start()

    @pl.when(has_next)
    def _():
        tail_copy.start()

    loads[3].wait()
    y_copies = []

    def pack(p, span, last_tile):
        base = p * share - p * share // 128 * 128
        for k in range(wide // 128):
            y_send[p, k * frames : (k + 1) * frames] = span[:, base + k * 128 : base + (k + 1) * 128]

    group = lax.broadcasted_iota(jnp.int32, (1, 128), 1) // rest
    left = jnp.zeros((frames, 128), F32)
    for p in range(parts - 1):
        tile0 = p * share // 128
        pack(p, yv[:, tile0 * 128 : (tile0 + 3) * 128], None)
        left = jnp.where(group == p, yv[:, (tile0 + 2) * 128 : (tile0 + 3) * 128].astype(F32), left)
    left_t = left.T.astype(BF16)
    for p in range(parts - 1):
        y_send[p, wide // 128 * frames :, :frames] = left_t[p * rest : (p + 1) * rest]

    for i in range(1, parts):
        to = lax.rem(t + i, parts)
        copy = remote(y_send.at[to], y_recv.at[i], (y_ss, y_rs), (i, i), tm=to)
        y_copies.append((to, copy))

        @pl.when(to < parts - 1)
        def _(copy=copy):
            copy.start()

    @pl.when(has_next)
    def _():
        rim_copy.wait_recv()

    @pl.when(jnp.logical_not(has_next))
    def _():
        rim_in[...] = jnp.zeros_like(rim_in)

    rim_y = rim_in[...]
    p = parts - 1
    tile0 = p * share // 128
    span = jnp.concatenate([yv[:, tile0 * 128 :], rim_y], 1)
    pack(p, span, None)
    y_send[p, wide // 128 * frames :, :frames] = rim_y.astype(F32).T.astype(BF16)[p * rest :]
    for to, copy in y_copies:

        @pl.when(to == parts - 1)
        def _(copy=copy):
            copy.start()

    loads[4].wait()
    foot = av[...]
    gram = dot(foot, foot, 0, 0)
    eye = lax.broadcasted_iota(jnp.int32, (neurons, neurons), 0) == lax.broadcasted_iota(
        jnp.int32, (neurons, neurons), 1
    )
    scale = jnp.sum(jnp.where(eye, gram, 0.0), 0, keepdims=True) + 1e-6
    own_drive = dot(jnp.concatenate([yv[...], rim_y], 1), foot)
    coupled = dot(start, gram, precision=lax.Precision.HIGHEST)
    base = own_drive - coupled

    @pl.when(has_next)
    def _():
        head_copy.wait_recv()

    @pl.when(has_prev)
    def _():
        tail_copy.wait_recv()

    @pl.when(jnp.logical_not(has_next))
    def _():
        head_in[...] = jnp.zeros_like(head_in)

    @pl.when(jnp.logical_not(has_prev))
    def _():
        tail_in[...] = jnp.zeros_like(tail_in)

    nh, nl = halves(head_in[...])
    ph, pw = halves(tail_in[...])
    outside = dot(
        jnp.concatenate([nh, nl, ph, pw], 1), jnp.concatenate([tail, tail, head, head], 0)
    )
    base = base - outside
    done = []
    for g in range(neurons // GROUP):
        cut = slice(g * GROUP, (g + 1) * GROUP)
        change = base[:, cut]
        for h in range(g):
            moved = done[h] - start[:, h * GROUP : (h + 1) * GROUP]
            change = change - dot(
                moved, gram[h * GROUP : (h + 1) * GROUP, cut], precision=lax.Precision.HIGHEST
            )
        done.append(
            jnp.where(
                live[:, cut], jnp.maximum(start[:, cut] + change / scale[:, cut], 0.0), 0.0
            )
        )
    new_tr = jnp.concatenate(done, 1)
    rounded = new_tr.astype(BF16)
    b_all[0] = rounded

    b_copies = []
    for i in range(1, parts):
        to = lax.rem(t + i, parts)
        copy = remote(b_all.at[0], b_all.at[i], (b_ss, b_rs), (i, i), tm=to)
        copy.start()
        b_copies.append(copy)

    side_head[...] = dot(rounded, head, 1, 1).astype(BF16)
    side_tail[...] = dot(rounded, tail, 1, 1).astype(BF16)
    to_first = lax.rem(parts - t, parts)
    to_last = parts - 1 - t
    tail_side = remote(
        side_tail, side_out.at[to_first], (s_ss, s_rs), (0, to_first), slab=s + 1, tm=t * 0
    )
    head_side = remote(
        side_head, side_out.at[to_last], (s_ss, s_rs), (1, to_last), slab=s - 1, tm=t * 0 + parts - 1
    )

    @pl.when(has_next)
    def _():
        tail_side.start()

    @pl.when(has_prev)
    def _():
        head_side.start()

    tr_out[...] = new_tr
    row0 = pl.multiple_of(t * share, 16)
    row = row0 + lax.broadcasted_iota(jnp.int32, (share, 1), 0)
    mine = av[pl.ds(row0, share)].astype(F32)
    share_out[...] = jnp.where(live & (row < rows), mine, 0.0).astype(BF16)

    y_recv[0] = y_send[t]
    for to, copy in y_copies:
        copy.wait_recv()
    per = wide // 128
    for k in range(per):
        block = y_recv[:, k * frames : (k + 1) * frames].reshape(parts * frames, 128)
        yt_out[k * 128 : (k + 1) * 128] = block.T
    yt_out[wide:] = jnp.concatenate(
        [y_recv[i, per * frames :, :frames] for i in range(parts)], 1
    )

    @pl.when((first & has_prev) | (last & has_next))
    def _():
        for i in range(parts):
            remote(side_tail, side_out.at[i], (s_ss, s_rs), (0, i), slab=s).wait_recv()

    @pl.when(jnp.logical_not((first & has_prev) | (last & has_next)))
    def _():
        side_out[...] = jnp.zeros_like(side_out)

    for copy in b_copies:
        copy.wait_recv()
    for to, copy in y_copies:
        copy.wait_send()
    for copy in b_copies:
        copy.wait_send()

    @pl.when(has_prev)
    def _():
        rim_copy.wait_send()
        head_copy.wait_send()
        head_side.wait_send()

    @pl.when(has_next)
    def _():
        tail_copy.wait_send()
        tail_side.wait_send()


def update_kernel(dims, live_ref, tr, b_all, yt, side, mine, tr_hbm, foot_out, delta, sem):
    slabs, parts, frames, voxels, rows, neurons = dims
    rim = rows - voxels
    share = rows // parts
    s = lax.axis_index("slab")
    t = lax.axis_index("tm")
    store = pltpu.make_async_copy(tr, tr_hbm, sem)
    store.start()
    live = lax.broadcasted_iota(jnp.int32, (1, neurons), 1) < live_ref[s]
    own = b_all[...].reshape(parts * frames, neurons)
    q = dot(own, own, 0, 0)
    delta[...] = dot(yt[...], own)

    @pl.when(t == 0)
    def _():
        delta[:rim] = delta[:rim] - dot(side[...].reshape(parts * frames, rim), own, 0, 0)

    @pl.when(t == parts - 1)
    def _():
        delta[share - rim :] = delta[share - rim :] - dot(
            side[...].reshape(parts * frames, rim), own, 0, 0
        )

    eye = lax.broadcasted_iota(jnp.int32, (neurons, neurons), 0) == lax.broadcasted_iota(
        jnp.int32, (neurons, neurons), 1
    )
    scale = jnp.maximum(jnp.sum(jnp.where(eye, q, 0.0), 0, keepdims=True), 1.0)
    q_high, q_low = halves(q)
    base = mine[...]
    coupling = dot(base, q_high) + dot(base, q_low)
    foot_out[...] = jnp.maximum(base.astype(F32) + (delta[...] - coupling) / scale, 0.0).astype(
        BF16
    )
    store.wait()


def solution(mesh):
    slabs, parts = mesh.shape["slab"], mesh.shape["tm"]

    def on_device(recording, footprints, traces, live_count):
        frames, voxels = recording.shape
        rows, neurons = footprints.shape
        rim = rows - voxels
        share = rows // parts
        dims = (slabs, parts, frames, voxels, rows, neurons)
        hbm = pl.BlockSpec(memory_space=pltpu.HBM)
        vmem = pl.BlockSpec(memory_space=pltpu.VMEM)
        smem = pl.BlockSpec(memory_space=pltpu.SMEM)
        packed = share // 128 * frames + share % 128
        dma = pltpu.SemaphoreType.DMA
        tr, b_all, yt, side, mine = pl.pallas_call(
            functools.partial(exchange_kernel, dims),
            out_shape=[
                pltpu.VMEM((frames, neurons), F32),
                pltpu.VMEM((parts, frames, neurons), BF16),
                pltpu.VMEM((share, parts * frames), BF16),
                pltpu.VMEM((parts, frames, rim), BF16),
                pltpu.VMEM((share, neurons), BF16),
            ],
            in_specs=[smem, hbm, hbm, hbm],
            out_specs=[vmem] * 5,
            scratch_shapes=[
                pltpu.VMEM((frames, voxels), BF16),
                pltpu.VMEM((rows, neurons), BF16),
                pltpu.VMEM((frames, neurons), F32),
                pltpu.VMEM((parts, packed, 128), BF16),
                pltpu.VMEM((parts, packed, 128), BF16),
                pltpu.VMEM((frames, rim), BF16),
                pltpu.VMEM((frames, rim), F32),
                pltpu.VMEM((frames, rim), F32),
                pltpu.VMEM((frames, rim), F32),
                pltpu.VMEM((frames, rim), F32),
                pltpu.VMEM((frames, rim), BF16),
                pltpu.VMEM((frames, rim), BF16),
                dma((5,)),
                dma((parts,)),
                dma((parts,)),
                dma((parts,)),
                dma((parts,)),
                dma((3,)),
                dma((3,)),
                dma((2,)),
                dma((parts,)),
            ],
            compiler_params=pltpu.CompilerParams(
                collective_id=0, has_side_effects=True, vmem_limit_bytes=32 * 2**20
            ),
            name="exchange",
        )(live_count, recording, footprints, traces)
        return pl.pallas_call(
            functools.partial(update_kernel, dims),
            out_shape=[
                jax.ShapeDtypeStruct((frames, neurons), F32),
                jax.ShapeDtypeStruct((share, neurons), BF16),
            ],
            in_specs=[smem] + [vmem] * 5,
            out_specs=[hbm, vmem],
            scratch_shapes=[pltpu.VMEM((share, neurons), F32), dma],
            compiler_params=pltpu.CompilerParams(vmem_limit_bytes=32 * 2**20),
            name="update",
        )(live_count, tr, b_all, yt, side, mine)

    placed = (P("tm", "slab"), P(None, "slab"), P("tm", "slab"), P())
    return jax.shard_map(
        on_device,
        mesh=mesh,
        in_specs=placed,
        out_specs=(P("tm", "slab"), P("tm", "slab")),
        check_vma=False,
    )
```

```python
import functools

import jax
import jax.numpy as jnp
from jax import lax
from jax.experimental import pallas as pl
from jax.experimental.pallas import tpu as pltpu
from jax.sharding import PartitionSpec as P

MESH = pl.DeviceIdType.MESH
F32 = jnp.float32
BF16 = jnp.bfloat16
GROUP = 128


def dot(a, b, ca=1, cb=0, precision=None):
    return lax.dot_general(
        a, b, (((ca,), (cb,)), ((), ())), preferred_element_type=F32, precision=precision
    )


def halves(x):
    high = x.astype(BF16)
    return high, (x - high.astype(F32)).astype(BF16)


def remote(src, dst, sems, index, **device):
    return pltpu.make_async_remote_copy(
        src_ref=src,
        dst_ref=dst,
        send_sem=sems[0].at[index[0]],
        recv_sem=sems[1].at[index[1]],
        device_id=device,
        device_id_type=MESH,
    )


def exchange_kernel(
    dims,
    live_ref, y_hbm, a_hbm, c_hbm,
    tr_out, b_all, yt_out, side_out, share_out,
    yv, av, cv, y_send, y_recv, rim_in, head_out, tail_out, head_in, tail_in,
    side_head, side_tail,
    load_sem, y_ss, y_rs, b_ss, b_rs, h_ss, h_rs, s_ss, s_rs,
):
    slabs, parts, frames, voxels, rows, neurons = dims
    rim = rows - voxels
    share = rows // parts
    wide = share // 128 * 128
    rest = share - wide
    s = lax.axis_index("slab")
    t = lax.axis_index("tm")
    has_next = s < slabs - 1
    has_prev = s > 0
    first, last = t == 0, t == parts - 1

    loads = [
        pltpu.make_async_copy(c_hbm, cv, load_sem.at[0]),
        pltpu.make_async_copy(a_hbm.at[:rim], av.at[:rim], load_sem.at[1]),
        pltpu.make_async_copy(a_hbm.at[voxels:], av.at[voxels:], load_sem.at[2]),
        pltpu.make_async_copy(y_hbm, yv, load_sem.at[3]),
        pltpu.make_async_copy(a_hbm.at[rim:voxels], av.at[rim:voxels], load_sem.at[4]),
    ]
    for load in loads:
        load.start()

    barrier = pltpu.get_barrier_semaphore()

    def greet(**device):
        pl.semaphore_signal(barrier, inc=1, device_id=device, device_id_type=MESH)

    for i in range(1, parts):
        greet(tm=lax.rem(t + i, parts))

    @pl.when(has_next)
    def _():
        greet(slab=s + 1)

    @pl.when(has_prev)
    def _():
        greet(slab=s - 1)

    @pl.when(first & has_prev)
    def _():
        for i in range(1, parts):
            greet(slab=s - 1, tm=t + i)

    @pl.when(last & has_next)
    def _():
        for i in range(1, parts):
            greet(slab=s + 1, tm=t - i)

    rim_copy = remote(y_hbm.at[:, :rim], rim_in, (h_ss, h_rs), (0, 0), slab=s - 1)
    head_copy = remote(head_out, head_in, (h_ss, h_rs), (1, 1), slab=s - 1)
    tail_copy = remote(tail_out, tail_in, (h_ss, h_rs), (2, 2), slab=s + 1)

    live = lax.broadcasted_iota(jnp.int32, (1, neurons), 1) < live_ref[s]
    for load in loads[:3]:
        load.wait()
    keep_tail = jnp.where(has_next, 1.0, 0.0).astype(F32)
    start = jnp.where(live, cv[...], 0.0)
    c_high, c_low = halves(start)
    head = av[:rim]
    tail = (av[voxels:].astype(F32) * keep_tail).astype(BF16)
    av[voxels:] = tail
    head_out[...] = dot(c_high, head, 1, 1) + dot(c_low, head, 1, 1)
    tail_out[...] = dot(c_high, tail, 1, 1) + dot(c_low, tail, 1, 1)

    one = jnp.int32(1)
    zero = jnp.int32(0)
    pl.semaphore_wait(
        barrier,
        parts - 1
        + jnp.where(has_next, jnp.where(first, one, one + 1), zero)
        + jnp.where(has_prev, jnp.where(last, one, one + 1), zero),
    )

    @pl.when(has_prev)
    def _():
        rim_copy.start()

    @pl.when(has_prev)
    def _():
        head_copy.start()

    @pl.when(has_next)
    def _():
        tail_copy.start()

    loads[3].wait()
    y_copies = []

    def pack(p, span, last_tile):
        base = p * share - p * share // 128 * 128
        for k in range(wide // 128):
            y_send[p, k * frames : (k + 1) * frames] = span[:, base + k * 128 : base + (k + 1) * 128]

    group = lax.broadcasted_iota(jnp.int32, (1, 128), 1) // rest
    left = jnp.zeros((frames, 128), F32)
    for p in range(parts - 1):
        tile0 = p * share // 128
        pack(p, yv[:, tile0 * 128 : (tile0 + 3) * 128], None)
        left = jnp.where(group == p, yv[:, (tile0 + 2) * 128 : (tile0 + 3) * 128].astype(F32), left)
    left_t = left.T.astype(BF16)
    for p in range(parts - 1):
        y_send[p, wide // 128 * frames :, :frames] = left_t[p * rest : (p + 1) * rest]

    across = t + 1 - 2 * lax.rem(t, 2)
    half = parts // 2
    routes = [(1, across)]
    routes += [(half + k, lax.rem(across + 2 * k, parts)) for k in range(1, half)]
    routes += [(1 + k, lax.rem(t + 2 * k, parts)) for k in range(1, half)]
    for i, to in routes:
        copy = remote(y_send.at[to], y_recv.at[i], (y_ss, y_rs), (i, i), tm=to)
        y_copies.append((to, copy))

        @pl.when(to < parts - 1)
        def _(copy=copy):
            copy.start()

    @pl.when(has_next)
    def _():
        rim_copy.wait_recv()

    @pl.when(jnp.logical_not(has_next))
    def _():
        rim_in[...] = jnp.zeros_like(rim_in)

    rim_y = rim_in[...]
    p = parts - 1
    tile0 = p * share // 128
    span = jnp.concatenate([yv[:, tile0 * 128 :], rim_y], 1)
    pack(p, span, None)
    y_send[p, wide // 128 * frames :, :frames] = rim_y.astype(F32).T.astype(BF16)[p * rest :]
    for to, copy in y_copies:

        @pl.when(to == parts - 1)
        def _(copy=copy):
            copy.start()

    loads[4].wait()
    foot = av[...]
    gram = dot(foot, foot, 0, 0)
    eye = lax.broadcasted_iota(jnp.int32, (neurons, neurons), 0) == lax.broadcasted_iota(
        jnp.int32, (neurons, neurons), 1
    )
    scale = jnp.sum(jnp.where(eye, gram, 0.0), 0, keepdims=True) + 1e-6
    own_drive = dot(jnp.concatenate([yv[...], rim_y], 1), foot)
    coupled = dot(start, gram, precision=lax.Precision.HIGHEST)
    base = own_drive - coupled

    @pl.when(has_next)
    def _():
        head_copy.wait_recv()

    @pl.when(has_prev)
    def _():
        tail_copy.wait_recv()

    @pl.when(jnp.logical_not(has_next))
    def _():
        head_in[...] = jnp.zeros_like(head_in)

    @pl.when(jnp.logical_not(has_prev))
    def _():
        tail_in[...] = jnp.zeros_like(tail_in)

    nh, nl = halves(head_in[...])
    ph, pw = halves(tail_in[...])
    outside = dot(
        jnp.concatenate([nh, nl, ph, pw], 1), jnp.concatenate([tail, tail, head, head], 0)
    )
    base = base - outside
    done = []
    for g in range(neurons // GROUP):
        cut = slice(g * GROUP, (g + 1) * GROUP)
        change = base[:, cut]
        for h in range(g):
            moved = done[h] - start[:, h * GROUP : (h + 1) * GROUP]
            change = change - dot(
                moved, gram[h * GROUP : (h + 1) * GROUP, cut], precision=lax.Precision.HIGHEST
            )
        done.append(
            jnp.where(
                live[:, cut], jnp.maximum(start[:, cut] + change / scale[:, cut], 0.0), 0.0
            )
        )
    new_tr = jnp.concatenate(done, 1)
    rounded = new_tr.astype(BF16)
    b_all[0] = rounded

    along = [lax.rem(t + i, parts) for i in range(2, parts, 2)]
    b_cross = remote(b_all.at[0], b_all.at[1], (b_ss, b_rs), (1, 1), tm=across)
    b_cross.start()
    b_copies = []
    for n, to in enumerate(along):
        copy = remote(b_all.at[0], b_all.at[2 + n], (b_ss, b_rs), (2 + n, 2 + n), tm=to)
        copy.start()
        b_copies.append(copy)

    side_head[...] = dot(rounded, head, 1, 1).astype(BF16)
    side_tail[...] = dot(rounded, tail, 1, 1).astype(BF16)
    def slot_at(x_to, z_to):
        away = lax.rem(x_to - t // 2 + parts, parts // 2)
        same, here = lax.rem(t, 2) == z_to, away == 0
        near = jnp.where(here, 0, 1 + away)
        far = jnp.where(here, 1, parts // 2 + away)
        return jnp.where(same, near, far)

    to_first = slot_at(0, 0)
    to_last = slot_at(parts // 2 - 1, 1)
    tail_side = remote(
        side_tail, side_out.at[to_first], (s_ss, s_rs), (0, to_first), slab=s + 1, tm=t * 0
    )
    head_side = remote(
        side_head, side_out.at[to_last], (s_ss, s_rs), (1, to_last), slab=s - 1, tm=t * 0 + parts - 1
    )

    @pl.when(has_next)
    def _():
        tail_side.start()

    @pl.when(has_prev)
    def _():
        head_side.start()

    tr_out[...] = new_tr
    b_cross.wait_recv()
    for n, to in enumerate(along):
        copy = remote(b_all.at[1], b_all.at[5 + n], (b_ss, b_rs), (5 + n, 5 + n), tm=to)
        copy.start()
        b_copies.append(copy)
    row0 = pl.multiple_of(t * share, 16)
    row = row0 + lax.broadcasted_iota(jnp.int32, (share, 1), 0)
    mine = av[pl.ds(row0, share)].astype(F32)
    share_out[...] = jnp.where(live & (row < rows), mine, 0.0).astype(BF16)

    y_recv[0] = y_send[t]
    for to, copy in y_copies:
        copy.wait_recv()
    per = wide // 128
    for k in range(per):
        block = y_recv[:, k * frames : (k + 1) * frames].reshape(parts * frames, 128)
        yt_out[k * 128 : (k + 1) * 128] = block.T
    yt_out[wide:] = jnp.concatenate(
        [y_recv[i, per * frames :, :frames] for i in range(parts)], 1
    )

    @pl.when((first & has_prev) | (last & has_next))
    def _():
        for i in range(parts):
            remote(side_tail, side_out.at[i], (s_ss, s_rs), (0, i), slab=s).wait_recv()

    @pl.when(jnp.logical_not((first & has_prev) | (last & has_next)))
    def _():
        side_out[...] = jnp.zeros_like(side_out)

    for copy in b_copies:
        copy.wait_recv()
    for to, copy in y_copies:
        copy.wait_send()
    b_cross.wait_send()
    for copy in b_copies:
        copy.wait_send()

    @pl.when(has_prev)
    def _():
        rim_copy.wait_send()
        head_copy.wait_send()
        head_side.wait_send()

    @pl.when(has_next)
    def _():
        tail_copy.wait_send()
        tail_side.wait_send()


def update_kernel(dims, live_ref, tr, b_all, yt, side, mine, tr_hbm, foot_out, delta, sem):
    slabs, parts, frames, voxels, rows, neurons = dims
    rim = rows - voxels
    share = rows // parts
    s = lax.axis_index("slab")
    t = lax.axis_index("tm")
    store = pltpu.make_async_copy(tr, tr_hbm, sem)
    store.start()
    live = lax.broadcasted_iota(jnp.int32, (1, neurons), 1) < live_ref[s]
    own = b_all[...].reshape(parts * frames, neurons)
    q = dot(own, own, 0, 0)
    delta[...] = dot(yt[...], own)

    @pl.when(t == 0)
    def _():
        delta[:rim] = delta[:rim] - dot(side[...].reshape(parts * frames, rim), own, 0, 0)

    @pl.when(t == parts - 1)
    def _():
        delta[share - rim :] = delta[share - rim :] - dot(
            side[...].reshape(parts * frames, rim), own, 0, 0
        )

    eye = lax.broadcasted_iota(jnp.int32, (neurons, neurons), 0) == lax.broadcasted_iota(
        jnp.int32, (neurons, neurons), 1
    )
    scale = jnp.maximum(jnp.sum(jnp.where(eye, q, 0.0), 0, keepdims=True), 1.0)
    q_high, q_low = halves(q)
    base = mine[...]
    coupling = dot(base, q_high) + dot(base, q_low)
    foot_out[...] = jnp.maximum(base.astype(F32) + (delta[...] - coupling) / scale, 0.0).astype(
        BF16
    )
    store.wait()


def solution(mesh):
    slabs, parts = mesh.shape["slab"], mesh.shape["tm"]

    def on_device(recording, footprints, traces, live_count):
        frames, voxels = recording.shape
        rows, neurons = footprints.shape
        rim = rows - voxels
        share = rows // parts
        dims = (slabs, parts, frames, voxels, rows, neurons)
        hbm = pl.BlockSpec(memory_space=pltpu.HBM)
        vmem = pl.BlockSpec(memory_space=pltpu.VMEM)
        smem = pl.BlockSpec(memory_space=pltpu.SMEM)
        packed = share // 128 * frames + share % 128
        dma = pltpu.SemaphoreType.DMA
        tr, b_all, yt, side, mine = pl.pallas_call(
            functools.partial(exchange_kernel, dims),
            out_shape=[
                pltpu.VMEM((frames, neurons), F32),
                pltpu.VMEM((parts, frames, neurons), BF16),
                pltpu.VMEM((share, parts * frames), BF16),
                pltpu.VMEM((parts, frames, rim), BF16),
                pltpu.VMEM((share, neurons), BF16),
            ],
            in_specs=[smem, hbm, hbm, hbm],
            out_specs=[vmem] * 5,
            scratch_shapes=[
                pltpu.VMEM((frames, voxels), BF16),
                pltpu.VMEM((rows, neurons), BF16),
                pltpu.VMEM((frames, neurons), F32),
                pltpu.VMEM((parts, packed, 128), BF16),
                pltpu.VMEM((parts, packed, 128), BF16),
                pltpu.VMEM((frames, rim), BF16),
                pltpu.VMEM((frames, rim), F32),
                pltpu.VMEM((frames, rim), F32),
                pltpu.VMEM((frames, rim), F32),
                pltpu.VMEM((frames, rim), F32),
                pltpu.VMEM((frames, rim), BF16),
                pltpu.VMEM((frames, rim), BF16),
                dma((5,)),
                dma((parts,)),
                dma((parts,)),
                dma((parts,)),
                dma((parts,)),
                dma((3,)),
                dma((3,)),
                dma((2,)),
                dma((parts,)),
            ],
            compiler_params=pltpu.CompilerParams(
                collective_id=0, has_side_effects=True, vmem_limit_bytes=60 * 2**20
            ),
            name="exchange",
        )(live_count, recording, footprints, traces)
        return pl.pallas_call(
            functools.partial(update_kernel, dims),
            out_shape=[
                jax.ShapeDtypeStruct((frames, neurons), F32),
                jax.ShapeDtypeStruct((share, neurons), BF16),
            ],
            in_specs=[smem] + [vmem] * 5,
            out_specs=[hbm, vmem],
            scratch_shapes=[pltpu.VMEM((share, neurons), F32), dma],
            compiler_params=pltpu.CompilerParams(vmem_limit_bytes=32 * 2**20),
            name="update",
        )(live_count, tr, b_all, yt, side, mine)

    placed = (P("tm", "slab"), P(None, "slab"), P("tm", "slab"), P())
    return jax.shard_map(
        on_device,
        mesh=mesh,
        in_specs=placed,
        out_specs=(P("tm", "slab"), P("tm", "slab")),
        check_vma=False,
    )
```

```python
import functools

import jax
import jax.numpy as jnp
from jax import lax
from jax.experimental import pallas as pl
from jax.experimental.pallas import tpu as pltpu
from jax.sharding import PartitionSpec as P

MESH = pl.DeviceIdType.MESH
F32 = jnp.float32
BF16 = jnp.bfloat16
GROUP = 128
LATE_CROSS = {4: 0, 5: 0, 6: 2, 7: 2}
EARLY_CROSS = 2
LATE_ALONG = 2


def dot(a, b, ca=1, cb=0, precision=None):
    return lax.dot_general(
        a, b, (((ca,), (cb,)), ((), ())), preferred_element_type=F32, precision=precision
    )


def halves(x):
    high = x.astype(BF16)
    return high, (x - high.astype(F32)).astype(BF16)


def remote(src, dst, sems, index, **device):
    return pltpu.make_async_remote_copy(
        src_ref=src,
        dst_ref=dst,
        send_sem=sems[0].at[index[0]],
        recv_sem=sems[1].at[index[1]],
        device_id=device,
        device_id_type=MESH,
    )


def exchange_kernel(
    dims,
    live_hbm, y_hbm, a_hbm, c_hbm,
    tr_out, b_all, yt_out, side_out, share_out,
    live_ref, yv, av, cv, y_send, y_recv, rim_in, head_out, tail_out, head_in, tail_in,
    side_head, side_tail,
    load_sem, y_ss, y_rs, b_ss, b_rs, h_ss, h_rs, s_ss, s_rs, ready, side_ready,
):
    slabs, parts, frames, voxels, rows, neurons = dims
    rim = rows - voxels
    share = rows // parts
    wide = share // 128 * 128
    rest = share - wide
    s = lax.axis_index("slab")
    t = lax.axis_index("tm")
    has_next = s < slabs - 1
    has_prev = s > 0
    first, last = t == 0, t == parts - 1
    early = lax.rem(t, 2) == 0
    late = jnp.logical_not(early)

    loads = [
        pltpu.make_async_copy(live_hbm, live_ref, load_sem.at[5]),
        pltpu.make_async_copy(c_hbm, cv, load_sem.at[0]),
        pltpu.make_async_copy(a_hbm.at[:rim], av.at[:rim], load_sem.at[1]),
        pltpu.make_async_copy(a_hbm.at[voxels:], av.at[voxels:], load_sem.at[2]),
        pltpu.make_async_copy(y_hbm, yv, load_sem.at[3]),
        pltpu.make_async_copy(a_hbm.at[rim:voxels], av.at[rim:voxels], load_sem.at[4]),
    ]
    barrier = pltpu.get_barrier_semaphore()

    def greet(**device):
        pl.semaphore_signal(barrier, inc=1, device_id=device, device_id_type=MESH)

    half = parts // 2
    across = t + 1 - 2 * lax.rem(t, 2)
    along = [lax.rem(t + 2 * k, parts) for k in range(1, half)]
    beyond = [across] + [lax.rem(across + 2 * k, parts) for k in range(1, half)]

    @pl.when(has_next)
    def _():
        greet(slab=s + 1)

    @pl.when(has_prev)
    def _():
        greet(slab=s - 1)

    for to in along:
        greet(tm=to)

    @pl.when(early)
    def _():
        for to in beyond:
            greet(tm=to)

    @pl.when(early & has_prev)
    def _():
        greet(slab=s - 1, tm=t * 0 + parts - 1)

    @pl.when(first & has_prev)
    def _():
        for i in range(1, parts - 1):
            greet(slab=s - 1, tm=t + i)

    for load in loads:
        load.start()

    rim_copy = remote(y_hbm.at[:, :rim], rim_in, (h_ss, h_rs), (0, 0), slab=s - 1)
    head_copy = remote(head_out, head_in, (h_ss, h_rs), (1, 1), slab=s - 1)
    tail_copy = remote(tail_out, tail_in, (h_ss, h_rs), (2, 2), slab=s + 1)

    for load in loads[:5]:
        load.wait()
    live = lax.broadcasted_iota(jnp.int32, (1, neurons), 1) < live_ref[s]
    keep_tail = jnp.where(has_next, 1.0, 0.0).astype(F32)
    start = jnp.where(live, cv[...], 0.0)
    c_high, c_low = halves(start)
    head = av[:rim]
    tail = (av[voxels:].astype(F32) * keep_tail).astype(BF16)
    av[voxels:] = tail
    head_out[...] = dot(c_high, head, 1, 1) + dot(c_low, head, 1, 1) - yv[:, :rim].astype(F32)
    tail_out[...] = dot(c_high, tail, 1, 1) + dot(c_low, tail, 1, 1)

    def count(condition, amount=1):
        return jnp.where(condition, jnp.int32(amount), jnp.int32(0))

    heard = half - 1 + count(has_next) + count(has_prev) + count(late, half)
    heard = heard + count(has_next & jnp.logical_not(first)) + count(last & has_next, half - 1)
    pl.semaphore_wait(barrier, heard)

    @pl.when(has_prev)
    def _():
        head_copy.start()

    @pl.when(has_next)
    def _():
        tail_copy.start()

    @pl.when(has_prev)
    def _():
        rim_copy.start()

    @pl.when(late)
    def _():
        for to in beyond:
            pl.semaphore_signal(ready, inc=1, device_id={"tm": to}, device_id_type=MESH)

    @pl.when(last & has_next)
    def _():
        for i in range(1, parts, 2):
            pl.semaphore_signal(
                side_ready, inc=1, device_id={"slab": s + 1, "tm": t - i}, device_id_type=MESH
            )

    y_copies = []

    def pack(p, span):
        base = p * share - p * share // 128 * 128
        for k in range(wide // 128):
            y_send[p, k * frames : (k + 1) * frames] = span[:, base + k * 128 : base + (k + 1) * 128]

    def pack_rest(p, columns):
        pair = jnp.concatenate([columns[: rest // 2], columns[rest // 2 :]], 1)
        y_send[p, wide // 128 * frames :] = pair.astype(BF16)

    group = lax.broadcasted_iota(jnp.int32, (1, 128), 1) // rest
    left = jnp.zeros((frames, 128), F32)
    for p in range(parts - 1):
        tile0 = p * share // 128
        pack(p, yv[:, tile0 * 128 : (tile0 + 3) * 128])
        left = jnp.where(group == p, yv[:, (tile0 + 2) * 128 : (tile0 + 3) * 128].astype(F32), left)
    left_t = left.T
    for p in range(parts - 1):
        pack_rest(p, left_t[p * rest : (p + 1) * rest])

    routes = list(enumerate(beyond, half)) + list(enumerate(along, 1))
    for i, to in routes:
        copy = remote(y_send.at[to], y_recv.at[i], (y_ss, y_rs), (i, i), tm=to)
        y_copies.append((i, to, copy))

    def send_shares(stage):
        for i, to, copy in y_copies:
            crossing = i >= half
            due = jnp.where(late, LATE_CROSS[i], EARLY_CROSS) if crossing else jnp.where(late, LATE_ALONG, 0)
            due = jnp.where(to == parts - 1, jnp.maximum(due, 2), due)

            @pl.when(due == stage)
            def _(copy=copy):
                copy.start()

    send_shares(0)

    loads[5].wait()
    foot = av[...]
    gram = dot(foot, foot, 0, 0)
    eye = lax.broadcasted_iota(jnp.int32, (neurons, neurons), 0) == lax.broadcasted_iota(
        jnp.int32, (neurons, neurons), 1
    )
    scale = jnp.sum(jnp.where(eye, gram, 0.0), 0, keepdims=True) + 1e-6
    own_drive = dot(yv[...], av[:voxels])
    coupled = dot(start, gram, precision=lax.Precision.HIGHEST)
    base = own_drive - coupled

    @pl.when(has_next)
    def _():
        head_copy.wait_recv()

    @pl.when(has_prev)
    def _():
        tail_copy.wait_recv()

    @pl.when(jnp.logical_not(has_next))
    def _():
        head_in[...] = jnp.zeros_like(head_in)

    @pl.when(jnp.logical_not(has_prev))
    def _():
        tail_in[...] = jnp.zeros_like(tail_in)

    nh, nl = halves(head_in[...])
    ph, pw = halves(tail_in[...])
    outside = dot(
        jnp.concatenate([nh, nl, ph, pw], 1), jnp.concatenate([tail, tail, head, head], 0)
    )
    base = base - outside
    done = []
    for g in range(neurons // GROUP):
        cut = slice(g * GROUP, (g + 1) * GROUP)
        change = base[:, cut]
        for h in range(g):
            moved = done[h] - start[:, h * GROUP : (h + 1) * GROUP]
            change = change - dot(
                moved, gram[h * GROUP : (h + 1) * GROUP, cut], precision=lax.Precision.HIGHEST
            )
        done.append(
            jnp.where(
                live[:, cut], jnp.maximum(start[:, cut] + change / scale[:, cut], 0.0), 0.0
            )
        )
    new_tr = jnp.concatenate(done, 1)
    rounded = new_tr.astype(BF16)
    b_all[0] = rounded

    b_cross = remote(b_all.at[0], b_all.at[half], (b_ss, b_rs), (half, half), tm=across)

    @pl.when(late)
    def _():
        b_cross.start()

    def slot_at(x_to, z_to):
        away = lax.rem(x_to - t // 2 + parts, half)
        return jnp.where(lax.rem(t, 2) == z_to, away, half + away)

    to_first = slot_at(0, 0)
    tail_side = remote(
        side_tail, side_out.at[to_first], (s_ss, s_rs), (0, to_first), slab=s + 1, tm=t * 0
    )
    to_last = slot_at(half - 1, 1)
    head_side = remote(
        side_head.at[0], side_out.at[to_last], (s_ss, s_rs), (1, to_last), slab=s - 1, tm=t * 0 + parts - 1
    )
    late_side = remote(
        side_head.at[pl.ds(1, half)], side_out.at[pl.ds(0, half)], (s_ss, s_rs), (2, parts), slab=s - 1
    )
    side_tail[...] = dot(rounded, tail, 1, 1).astype(BF16)

    @pl.when(has_next)
    def _():
        tail_side.start()

    b_copies = []
    for k, to in enumerate(along, 1):
        copy = remote(b_all.at[0], b_all.at[k], (b_ss, b_rs), (k, k), tm=to)
        copy.start()
        b_copies.append(copy)

    @pl.when(has_next)
    def _():
        rim_copy.wait_recv()

    @pl.when(jnp.logical_not(has_next))
    def _():
        rim_in[...] = jnp.zeros_like(rim_in)

    rim_y = rim_in[...]
    p = parts - 1
    tile0 = p * share // 128
    span = jnp.concatenate([yv[:, tile0 * 128 :], rim_y], 1)
    pack(p, span)
    pack_rest(p, rim_y.astype(F32).T[p * rest :])
    @pl.when(early)
    def _():
        pl.semaphore_wait(ready, half)
        b_cross.start()

    send_shares(2)
    tr_out[...] = new_tr

    @pl.when(last & has_prev)
    def _():
        for copy in b_copies:
            copy.wait_recv()
        odd = b_all[:half].reshape(half * frames, neurons)
        side_head[1:] = dot(odd, av[:rim], 1, 1).astype(BF16).reshape(half, frames, rim)
        late_side.start()

    @pl.when(jnp.logical_not(last & has_prev))
    def _():
        side_head[0] = dot(rounded, head, 1, 1).astype(BF16)

    b_cross.wait_recv()
    passed = []
    for k, to in enumerate(along, 1):
        copy = remote(b_all.at[half], b_all.at[half + k], (b_ss, b_rs), (half + k, half + k), tm=to)
        copy.start()
        passed.append(copy)

    @pl.when(early & has_prev)
    def _():
        pl.semaphore_wait(side_ready, 1)
        head_side.start()

    send_shares(3)
    row0 = pl.multiple_of(t * share, 16)
    row = row0 + lax.broadcasted_iota(jnp.int32, (share, 1), 0)
    mine = av[pl.ds(row0, share)].astype(F32)
    share_out[...] = jnp.where(live & (row < rows), mine, 0.0).astype(BF16)

    y_recv[0] = y_send[t]
    for _, _, copy in y_copies:
        copy.wait_recv()
    per = wide // 128
    for k in range(per):
        block = y_recv[:, k * frames : (k + 1) * frames].reshape(parts * frames, 128)
        yt_out[k * 128 : (k + 1) * 128] = block.T
    pairs = [y_recv[i, per * frames :].astype(F32) for i in range(parts)]
    yt_out[wide:] = jnp.concatenate(
        [jnp.concatenate([q[:, :frames] for q in pairs], 1), jnp.concatenate([q[:, frames:] for q in pairs], 1)], 0
    ).astype(BF16)

    @pl.when(jnp.logical_not(last & has_prev))
    def _():
        for copy in b_copies:
            copy.wait_recv()

    for copy in passed:
        copy.wait_recv()

    @pl.when(first & has_prev)
    def _():
        for i in range(parts):
            remote(side_tail, side_out.at[i], (s_ss, s_rs), (0, i), slab=s).wait_recv()

    @pl.when(last & has_next)
    def _():
        late_side.wait_recv()
        for i in range(half, parts):
            remote(side_tail, side_out.at[i], (s_ss, s_rs), (0, i), slab=s).wait_recv()

    for _, _, copy in y_copies:
        copy.wait_send()
    b_cross.wait_send()
    for copy in b_copies + passed:
        copy.wait_send()

    @pl.when(has_prev)
    def _():
        rim_copy.wait_send()
        head_copy.wait_send()

    @pl.when(early & has_prev)
    def _():
        head_side.wait_send()

    @pl.when(last & has_prev)
    def _():
        late_side.wait_send()

    @pl.when(has_next)
    def _():
        tail_copy.wait_send()
        tail_side.wait_send()


def update_kernel(dims, tr, b_all, yt, side, mine, tr_hbm, foot_out, delta, sem):
    slabs, parts, frames, voxels, rows, neurons = dims
    rim = rows - voxels
    share = rows // parts
    s = lax.axis_index("slab")
    t = lax.axis_index("tm")
    store = pltpu.make_async_copy(tr, tr_hbm, sem)
    store.start()
    own = b_all[...].reshape(parts * frames, neurons)
    q = dot(own, own, 0, 0)
    delta[...] = dot(yt[...], own)

    @pl.when((t == 0) & (s > 0))
    def _():
        delta[:rim] = delta[:rim] - dot(side[...].reshape(parts * frames, rim), own, 0, 0)

    @pl.when((t == parts - 1) & (s < slabs - 1))
    def _():
        delta[share - rim :] = delta[share - rim :] - dot(
            side[...].reshape(parts * frames, rim), own, 0, 0
        )

    eye = lax.broadcasted_iota(jnp.int32, (neurons, neurons), 0) == lax.broadcasted_iota(
        jnp.int32, (neurons, neurons), 1
    )
    scale = jnp.maximum(jnp.sum(jnp.where(eye, q, 0.0), 0, keepdims=True), 1.0)
    q_high, q_low = halves(q)
    base = mine[...]
    coupling = dot(base, q_high) + dot(base, q_low)
    foot_out[...] = jnp.maximum(base.astype(F32) + (delta[...] - coupling) / scale, 0.0).astype(
        BF16
    )
    store.wait()


def solution(mesh):
    slabs, parts = mesh.shape["slab"], mesh.shape["tm"]

    def on_device(recording, footprints, traces, live_count):
        frames, voxels = recording.shape
        rows, neurons = footprints.shape
        rim = rows - voxels
        share = rows // parts
        half = parts // 2
        dims = (slabs, parts, frames, voxels, rows, neurons)
        hbm = pl.BlockSpec(memory_space=pltpu.HBM)
        vmem = pl.BlockSpec(memory_space=pltpu.VMEM)
        packed = share // 128 * frames + share % 128 // 2
        dma = pltpu.SemaphoreType.DMA
        tr, b_all, yt, side, mine = pl.pallas_call(
            functools.partial(exchange_kernel, dims),
            out_shape=[
                pltpu.VMEM((frames, neurons), F32),
                pltpu.VMEM((parts, frames, neurons), BF16),
                pltpu.VMEM((share, parts * frames), BF16),
                pltpu.VMEM((parts, frames, rim), BF16),
                pltpu.VMEM((share, neurons), BF16),
            ],
            in_specs=[hbm, hbm, hbm, hbm],
            out_specs=[vmem] * 5,
            scratch_shapes=[
                pltpu.SMEM((slabs,), jnp.int32),
                pltpu.VMEM((frames, voxels), BF16),
                pltpu.VMEM((rows, neurons), BF16),
                pltpu.VMEM((frames, neurons), F32),
                pltpu.VMEM((parts, packed, 128), BF16),
                pltpu.VMEM((parts, packed, 128), BF16),
                pltpu.VMEM((frames, rim), BF16),
                pltpu.VMEM((frames, rim), F32),
                pltpu.VMEM((frames, rim), F32),
                pltpu.VMEM((frames, rim), F32),
                pltpu.VMEM((frames, rim), F32),
                pltpu.VMEM((half + 1, frames, rim), BF16),
                pltpu.VMEM((frames, rim), BF16),
                dma((6,)),
                dma((parts,)),
                dma((parts,)),
                dma((parts,)),
                dma((parts,)),
                dma((3,)),
                dma((3,)),
                dma((3,)),
                dma((parts + 1,)),
                pltpu.SemaphoreType.REGULAR,
                pltpu.SemaphoreType.REGULAR,
            ],
            compiler_params=pltpu.CompilerParams(
                collective_id=0, has_side_effects=True, vmem_limit_bytes=60 * 2**20
            ),
            name="exchange",
        )(live_count, recording, footprints, traces)
        return pl.pallas_call(
            functools.partial(update_kernel, dims),
            out_shape=[
                jax.ShapeDtypeStruct((frames, neurons), F32),
                jax.ShapeDtypeStruct((share, neurons), BF16),
            ],
            in_specs=[vmem] * 5,
            out_specs=[hbm, vmem],
            scratch_shapes=[pltpu.VMEM((share, neurons), F32), dma],
            compiler_params=pltpu.CompilerParams(vmem_limit_bytes=32 * 2**20),
            name="update",
        )(tr, b_all, yt, side, mine)

    placed = (P("tm", "slab"), P(None, "slab"), P("tm", "slab"), P())
    return jax.shard_map(
        on_device,
        mesh=mesh,
        in_specs=placed,
        out_specs=(P("tm", "slab"), P("tm", "slab")),
        check_vma=False,
    )
```

```python
import functools

import jax
import jax.numpy as jnp
from jax import lax
from jax.experimental import pallas as pl
from jax.experimental.pallas import tpu as pltpu
from jax.sharding import PartitionSpec as P

MESH = pl.DeviceIdType.MESH
F32 = jnp.float32
BF16 = jnp.bfloat16
GROUP = 128
LATE_CROSS = ((0, 0, 2, 2), (0, 0, 0, 2), (0, 0, 0, 2), (0, 2, 2, 2))
EARLY_CROSS = 2
LATE_ALONG = 2


def dot(a, b, ca=1, cb=0, precision=None):
    return lax.dot_general(
        a, b, (((ca,), (cb,)), ((), ())), preferred_element_type=F32, precision=precision
    )


def halves(x):
    high = x.astype(BF16)
    return high, (x - high.astype(F32)).astype(BF16)


def remote(src, dst, sems, index, **device):
    return pltpu.make_async_remote_copy(
        src_ref=src,
        dst_ref=dst,
        send_sem=sems[0].at[index[0]],
        recv_sem=sems[1].at[index[1]],
        device_id=device,
        device_id_type=MESH,
    )


def exchange_kernel(
    dims,
    live_hbm, y_hbm, a_hbm, c_hbm,
    tr_out, b_all, yt_out, side_out, share_out, q_part, m_part,
    live_ref, yv, av, cv, y_send, y_recv, rim_in, head_out, tail_out, head_in, tail_in,
    side_head, side_tail,
    load_sem, y_ss, y_rs, b_ss, b_rs, h_ss, h_rs, s_ss, s_rs, ready, side_ready,
):
    slabs, parts, frames, voxels, rows, neurons = dims
    rim = rows - voxels
    share = rows // parts
    wide = share // 128 * 128
    rest = share - wide
    s = lax.axis_index("slab")
    t = lax.axis_index("tm")
    has_next = s < slabs - 1
    has_prev = s > 0
    first, last = t == 0, t == parts - 1
    early = lax.rem(t, 2) == 0
    late = jnp.logical_not(early)

    loads = [
        pltpu.make_async_copy(live_hbm, live_ref, load_sem.at[5]),
        pltpu.make_async_copy(c_hbm, cv, load_sem.at[0]),
        pltpu.make_async_copy(a_hbm.at[:rim], av.at[:rim], load_sem.at[1]),
        pltpu.make_async_copy(a_hbm.at[voxels:], av.at[voxels:], load_sem.at[2]),
        pltpu.make_async_copy(y_hbm, yv, load_sem.at[3]),
        pltpu.make_async_copy(a_hbm.at[rim:voxels], av.at[rim:voxels], load_sem.at[4]),
    ]
    barrier = pltpu.get_barrier_semaphore()

    def greet(**device):
        pl.semaphore_signal(barrier, inc=1, device_id=device, device_id_type=MESH)

    half = parts // 2
    across = t + 1 - 2 * lax.rem(t, 2)
    along = [lax.rem(t + 2 * k, parts) for k in range(1, half)]
    beyond = [across] + [lax.rem(across + 2 * k, parts) for k in range(1, half)]

    @pl.when(has_next)
    def _():
        greet(slab=s + 1)

    @pl.when(has_prev)
    def _():
        greet(slab=s - 1)

    for to in along:
        greet(tm=to)

    @pl.when(early)
    def _():
        for to in beyond:
            greet(tm=to)

    @pl.when(early & has_prev)
    def _():
        greet(slab=s - 1, tm=t * 0 + parts - 1)

    @pl.when(first & has_prev)
    def _():
        for i in range(1, parts - 1):
            greet(slab=s - 1, tm=t + i)

    for load in loads:
        load.start()

    rim_copy = remote(y_hbm.at[:, :rim], rim_in, (h_ss, h_rs), (0, 0), slab=s - 1)
    head_copy = remote(head_out, head_in, (h_ss, h_rs), (1, 1), slab=s - 1)
    tail_copy = remote(tail_out, tail_in, (h_ss, h_rs), (2, 2), slab=s + 1)

    for load in loads[:5]:
        load.wait()
    live = lax.broadcasted_iota(jnp.int32, (1, neurons), 1) < live_ref[s]
    keep_tail = jnp.where(has_next, 1.0, 0.0).astype(F32)
    start = jnp.where(live, cv[...], 0.0)
    c_high, c_low = halves(start)
    head = av[:rim]
    tail = (av[voxels:].astype(F32) * keep_tail).astype(BF16)
    av[voxels:] = tail
    head_out[...] = dot(c_high, head, 1, 1) + dot(c_low, head, 1, 1) - yv[:, :rim].astype(F32)
    tail_out[...] = dot(c_high, tail, 1, 1) + dot(c_low, tail, 1, 1)

    def count(condition, amount=1):
        return jnp.where(condition, jnp.int32(amount), jnp.int32(0))

    heard = half - 1 + count(has_next) + count(has_prev) + count(late, half)
    heard = heard + count(has_next & jnp.logical_not(first)) + count(last & has_next, half - 1)
    pl.semaphore_wait(barrier, heard)

    @pl.when(has_prev)
    def _():
        head_copy.start()

    @pl.when(has_next)
    def _():
        tail_copy.start()

    @pl.when(has_prev)
    def _():
        rim_copy.start()

    @pl.when(late)
    def _():
        for to in beyond:
            pl.semaphore_signal(ready, inc=1, device_id={"tm": to}, device_id_type=MESH)

    @pl.when(last & has_next)
    def _():
        for i in range(1, parts, 2):
            pl.semaphore_signal(
                side_ready, inc=1, device_id={"slab": s + 1, "tm": t - i}, device_id_type=MESH
            )

    y_copies = []

    def pack(p, span):
        base = p * share - p * share // 128 * 128
        for k in range(wide // 128):
            y_send[p, k * frames : (k + 1) * frames] = span[:, base + k * 128 : base + (k + 1) * 128]

    def pack_rest(p, columns):
        pair = jnp.concatenate([columns[: rest // 2], columns[rest // 2 :]], 1)
        y_send[p, wide // 128 * frames :] = pair.astype(BF16)

    group = lax.broadcasted_iota(jnp.int32, (1, 128), 1) // rest
    left = jnp.zeros((frames, 128), F32)
    for p in range(parts - 1):
        tile0 = p * share // 128
        pack(p, yv[:, tile0 * 128 : (tile0 + 3) * 128])
        left = jnp.where(group == p, yv[:, (tile0 + 2) * 128 : (tile0 + 3) * 128].astype(F32), left)
    left_t = left.T
    for p in range(parts - 1):
        pack_rest(p, left_t[p * rest : (p + 1) * rest])

    routes = list(enumerate(beyond, half)) + list(enumerate(along, 1))
    for i, to in routes:
        copy = remote(y_send.at[to], y_recv.at[i], (y_ss, y_rs), (i, i), tm=to)
        y_copies.append((i, to, copy))

    def send_shares(stage):
        for i, to, copy in y_copies:
            crossing = i >= half
            if crossing:
                due = jnp.int32(LATE_CROSS[0][i - half])
                for zone, stages in enumerate(LATE_CROSS):
                    due = jnp.where(s * len(LATE_CROSS) // slabs == zone, stages[i - half], due)
                due = jnp.where(late, jnp.where(to == 0, 0, due), EARLY_CROSS)
            else:
                due = jnp.where(late, LATE_ALONG, 0)
            due = jnp.where(to == parts - 1, jnp.maximum(due, 2), due)

            @pl.when(due == stage)
            def _(copy=copy):
                copy.start()

    send_shares(0)

    loads[5].wait()
    foot = av[...]
    gram = dot(foot, foot, 0, 0)
    eye = lax.broadcasted_iota(jnp.int32, (neurons, neurons), 0) == lax.broadcasted_iota(
        jnp.int32, (neurons, neurons), 1
    )
    scale = jnp.sum(jnp.where(eye, gram, 0.0), 0, keepdims=True) + 1e-6
    own_drive = dot(yv[...], av[:voxels])
    coupled = dot(start, gram, precision=lax.Precision.HIGHEST)
    base = own_drive - coupled

    @pl.when(has_next)
    def _():
        head_copy.wait_recv()

    @pl.when(has_prev)
    def _():
        tail_copy.wait_recv()

    @pl.when(jnp.logical_not(has_next))
    def _():
        head_in[...] = jnp.zeros_like(head_in)

    @pl.when(jnp.logical_not(has_prev))
    def _():
        tail_in[...] = jnp.zeros_like(tail_in)

    nh, nl = halves(head_in[...])
    ph, pw = halves(tail_in[...])
    outside = dot(
        jnp.concatenate([nh, nl, ph, pw], 1), jnp.concatenate([tail, tail, head, head], 0)
    )
    base = base - outside
    done = []
    for g in range(neurons // GROUP):
        cut = slice(g * GROUP, (g + 1) * GROUP)
        change = base[:, cut]
        for h in range(g):
            moved = done[h] - start[:, h * GROUP : (h + 1) * GROUP]
            change = change - dot(
                moved, gram[h * GROUP : (h + 1) * GROUP, cut], precision=lax.Precision.HIGHEST
            )
        done.append(
            jnp.where(
                live[:, cut], jnp.maximum(start[:, cut] + change / scale[:, cut], 0.0), 0.0
            )
        )
    new_tr = jnp.concatenate(done, 1)
    rounded = new_tr.astype(BF16)
    b_all[0] = rounded

    b_cross = remote(b_all.at[0], b_all.at[half], (b_ss, b_rs), (half, half), tm=across)

    @pl.when(late)
    def _():
        b_cross.start()

    def slot_at(x_to, z_to):
        away = lax.rem(x_to - t // 2 + parts, half)
        return jnp.where(lax.rem(t, 2) == z_to, away, half + away)

    to_first = slot_at(0, 0)
    tail_side = remote(
        side_tail, side_out.at[to_first], (s_ss, s_rs), (0, to_first), slab=s + 1, tm=t * 0
    )
    to_last = slot_at(half - 1, 1)
    head_side = remote(
        side_head.at[0], side_out.at[to_last], (s_ss, s_rs), (1, to_last), slab=s - 1, tm=t * 0 + parts - 1
    )
    late_side = remote(
        side_head.at[pl.ds(1, half)], side_out.at[pl.ds(0, half)], (s_ss, s_rs), (2, parts), slab=s - 1
    )
    side_tail[...] = dot(rounded, tail, 1, 1).astype(BF16)

    @pl.when(has_next)
    def _():
        tail_side.start()

    b_copies = []
    for k, to in enumerate(along, 1):
        copy = remote(b_all.at[0], b_all.at[k], (b_ss, b_rs), (k, k), tm=to)
        copy.start()
        b_copies.append(copy)

    @pl.when(has_next)
    def _():
        rim_copy.wait_recv()

    @pl.when(jnp.logical_not(has_next))
    def _():
        rim_in[...] = jnp.zeros_like(rim_in)

    rim_y = rim_in[...]
    p = parts - 1
    tile0 = p * share // 128
    span = jnp.concatenate([yv[:, tile0 * 128 :], rim_y], 1)
    pack(p, span)
    pack_rest(p, rim_y.astype(F32).T[p * rest :])
    @pl.when(early)
    def _():
        pl.semaphore_wait(ready, half)
        b_cross.start()

    send_shares(2)
    tr_out[...] = new_tr

    @pl.when(last & has_prev)
    def _():
        for copy in b_copies:
            copy.wait_recv()
        odd = b_all[:half].reshape(half * frames, neurons)
        side_head[1:] = dot(odd, av[:rim], 1, 1).astype(BF16).reshape(half, frames, rim)
        late_side.start()

    @pl.when(jnp.logical_not(last & has_prev))
    def _():
        side_head[0] = dot(rounded, head, 1, 1).astype(BF16)

    b_cross.wait_recv()
    passed = []
    for k, to in enumerate(along, 1):
        copy = remote(b_all.at[half], b_all.at[half + k], (b_ss, b_rs), (half + k, half + k), tm=to)
        copy.start()
        passed.append(copy)

    @pl.when(early & has_prev)
    def _():
        pl.semaphore_wait(side_ready, 1)
        head_side.start()

    send_shares(3)
    row0 = pl.multiple_of(t * share, 16)
    row = row0 + lax.broadcasted_iota(jnp.int32, (share, 1), 0)
    mine = av[pl.ds(row0, share)].astype(F32)
    share_out[...] = jnp.where(live & (row < rows), mine, 0.0).astype(BF16)

    per = wide // 128

    def voxels_first(base):
        tiles = [
            y_recv[base : base + half, k * frames : (k + 1) * frames].reshape(half * frames, 128).T
            for k in range(per)
        ]
        pairs = [y_recv[base + i, per * frames :].astype(F32) for i in range(half)]
        low = jnp.concatenate([q[:, :frames] for q in pairs], 1)
        high = jnp.concatenate([q[:, frames:] for q in pairs], 1)
        return jnp.concatenate(tiles + [jnp.concatenate([low, high], 0).astype(BF16)], 0)

    y_recv[0] = y_send[t]
    for i, _, copy in y_copies:
        if i < half:
            copy.wait_recv()

    @pl.when(jnp.logical_not(last & has_prev))
    def _():
        for copy in b_copies:
            copy.wait_recv()

    near = b_all[:half].reshape(half * frames, neurons)
    q_part[...] = dot(near, near, 0, 0)
    m_part[...] = dot(voxels_first(0), near)

    @pl.when(first & has_prev)
    def _():
        for i in range(half):
            remote(side_tail, side_out.at[i], (s_ss, s_rs), (0, i), slab=s).wait_recv()
        sides = side_out[:half].reshape(half * frames, rim)
        m_part[:rim] = m_part[:rim] - dot(sides, near, 0, 0)

    @pl.when(last & has_next)
    def _():
        late_side.wait_recv()
        sides = side_out[:half].reshape(half * frames, rim)
        m_part[share - rim :] = m_part[share - rim :] - dot(sides, near, 0, 0)

    for i, _, copy in y_copies:
        if i >= half:
            copy.wait_recv()
    yt_out[...] = voxels_first(half)
    for copy in passed:
        copy.wait_recv()

    @pl.when((first & has_prev) | (last & has_next))
    def _():
        for i in range(half, parts):
            remote(side_tail, side_out.at[i], (s_ss, s_rs), (0, i), slab=s).wait_recv()

    for _, _, copy in y_copies:
        copy.wait_send()
    b_cross.wait_send()
    for copy in b_copies + passed:
        copy.wait_send()

    @pl.when(has_prev)
    def _():
        rim_copy.wait_send()
        head_copy.wait_send()

    @pl.when(early & has_prev)
    def _():
        head_side.wait_send()

    @pl.when(last & has_prev)
    def _():
        late_side.wait_send()

    @pl.when(has_next)
    def _():
        tail_copy.wait_send()
        tail_side.wait_send()


def update_kernel(dims, tr, b_all, yt, side, mine, q_part, m_part, tr_hbm, foot_hbm, delta, foot, sems):
    slabs, parts, frames, voxels, rows, neurons = dims
    rim = rows - voxels
    share = rows // parts
    half = parts // 2
    s = lax.axis_index("slab")
    t = lax.axis_index("tm")
    stores = [pltpu.make_async_copy(tr, tr_hbm, sems.at[0])]
    stores[0].start()
    far = b_all[half:].reshape(half * frames, neurons)
    q = q_part[...] + dot(far, far, 0, 0)
    delta[...] = m_part[...] + dot(yt[...], far)

    @pl.when((t == 0) & (s > 0))
    def _():
        delta[:rim] = delta[:rim] - dot(side[half:].reshape(half * frames, rim), far, 0, 0)

    @pl.when((t == parts - 1) & (s < slabs - 1))
    def _():
        delta[share - rim :] = delta[share - rim :] - dot(
            side[half:].reshape(half * frames, rim), far, 0, 0
        )

    eye = lax.broadcasted_iota(jnp.int32, (neurons, neurons), 0) == lax.broadcasted_iota(
        jnp.int32, (neurons, neurons), 1
    )
    scale = jnp.maximum(jnp.sum(jnp.where(eye, q, 0.0), 0, keepdims=True), 1.0)
    q_high, q_low = halves(q)
    cut = share // 32 * 16
    for n, span in enumerate((slice(0, cut), slice(cut, share))):
        base = mine[span]
        coupling = dot(base, q_high) + dot(base, q_low)
        foot[span] = jnp.maximum(
            base.astype(F32) + (delta[span] - coupling) / scale, 0.0
        ).astype(BF16)
        store = pltpu.make_async_copy(foot.at[span], foot_hbm.at[span], sems.at[1 + n])
        store.start()
        stores.append(store)
    for store in stores:
        store.wait()


def solution(mesh):
    slabs, parts = mesh.shape["slab"], mesh.shape["tm"]

    def on_device(recording, footprints, traces, live_count):
        frames, voxels = recording.shape
        rows, neurons = footprints.shape
        rim = rows - voxels
        share = rows // parts
        half = parts // 2
        dims = (slabs, parts, frames, voxels, rows, neurons)
        hbm = pl.BlockSpec(memory_space=pltpu.HBM)
        vmem = pl.BlockSpec(memory_space=pltpu.VMEM)
        packed = share // 128 * frames + share % 128 // 2
        dma = pltpu.SemaphoreType.DMA
        tr, b_all, yt, side, mine, q_part, m_part = pl.pallas_call(
            functools.partial(exchange_kernel, dims),
            out_shape=[
                pltpu.VMEM((frames, neurons), F32),
                pltpu.VMEM((parts, frames, neurons), BF16),
                pltpu.VMEM((share, half * frames), BF16),
                pltpu.VMEM((parts, frames, rim), BF16),
                pltpu.VMEM((share, neurons), BF16),
                pltpu.VMEM((neurons, neurons), F32),
                pltpu.VMEM((share, neurons), F32),
            ],
            in_specs=[hbm, hbm, hbm, hbm],
            out_specs=[vmem] * 7,
            scratch_shapes=[
                pltpu.SMEM((slabs,), jnp.int32),
                pltpu.VMEM((frames, voxels), BF16),
                pltpu.VMEM((rows, neurons), BF16),
                pltpu.VMEM((frames, neurons), F32),
                pltpu.VMEM((parts, packed, 128), BF16),
                pltpu.VMEM((parts, packed, 128), BF16),
                pltpu.VMEM((frames, rim), BF16),
                pltpu.VMEM((frames, rim), F32),
                pltpu.VMEM((frames, rim), F32),
                pltpu.VMEM((frames, rim), F32),
                pltpu.VMEM((frames, rim), F32),
                pltpu.VMEM((half + 1, frames, rim), BF16),
                pltpu.VMEM((frames, rim), BF16),
                dma((6,)),
                dma((parts,)),
                dma((parts,)),
                dma((parts,)),
                dma((parts,)),
                dma((3,)),
                dma((3,)),
                dma((3,)),
                dma((parts + 1,)),
                pltpu.SemaphoreType.REGULAR,
                pltpu.SemaphoreType.REGULAR,
            ],
            compiler_params=pltpu.CompilerParams(
                collective_id=0, has_side_effects=True, vmem_limit_bytes=60 * 2**20
            ),
            name="exchange",
        )(live_count, recording, footprints, traces)
        return pl.pallas_call(
            functools.partial(update_kernel, dims),
            out_shape=[
                jax.ShapeDtypeStruct((frames, neurons), F32),
                jax.ShapeDtypeStruct((share, neurons), BF16),
            ],
            in_specs=[vmem] * 7,
            out_specs=[hbm, hbm],
            scratch_shapes=[
                pltpu.VMEM((share, neurons), F32),
                pltpu.VMEM((share, neurons), BF16),
                dma((3,)),
            ],
            compiler_params=pltpu.CompilerParams(vmem_limit_bytes=32 * 2**20),
            name="update",
        )(tr, b_all, yt, side, mine, q_part, m_part)

    placed = (P("tm", "slab"), P(None, "slab"), P("tm", "slab"), P())
    return jax.shard_map(
        on_device,
        mesh=mesh,
        in_specs=placed,
        out_specs=(P("tm", "slab"), P("tm", "slab")),
        check_vma=False,
    )
```

```python
import functools

import jax
import jax.numpy as jnp
from jax import lax
from jax.experimental import pallas as pl
from jax.experimental.pallas import tpu as pltpu
from jax.sharding import PartitionSpec as P

MESH = pl.DeviceIdType.MESH
F32 = jnp.float32
BF16 = jnp.bfloat16
GROUP = 128
LATE_CROSS = ((0, 0, 2, 2), (0, 0, 0, 2), (0, 0, 0, 2), (0, 2, 2, 2))
EARLY_CROSS = 2
PATIENT = 2


def dot(a, b, ca=1, cb=0, precision=None):
    return lax.dot_general(
        a, b, (((ca,), (cb,)), ((), ())), preferred_element_type=F32, precision=precision
    )


def halves(x):
    high = x.astype(BF16)
    return high, (x - high.astype(F32)).astype(BF16)


def remote(src, dst, sems, index, **device):
    return pltpu.make_async_remote_copy(
        src_ref=src,
        dst_ref=dst,
        send_sem=sems[0].at[index[0]],
        recv_sem=sems[1].at[index[1]],
        device_id=device,
        device_id_type=MESH,
    )


def exchange_kernel(
    dims,
    live_hbm, y_hbm, a_hbm, c_hbm,
    tr_out, b_all, yt_out, side_out, share_out, q_part, m_part,
    live_ref, yv, av, cv, y_send, y_recv, rim_in, head_out, tail_out, head_in, tail_in,
    side_head, side_tail,
    load_sem, y_ss, y_rs, b_ss, b_rs, h_ss, h_rs, s_ss, s_rs, ready, side_ready,
):
    slabs, parts, frames, voxels, rows, neurons = dims
    rim = rows - voxels
    share = rows // parts
    wide = share // 128 * 128
    rest = share - wide
    s = lax.axis_index("slab")
    t = lax.axis_index("tm")
    has_next = s < slabs - 1
    has_prev = s > 0
    first, last = t == 0, t == parts - 1
    early = lax.rem(t, 2) == 0
    late = jnp.logical_not(early)
    patient = late & (s * len(LATE_CROSS) // slabs < PATIENT)

    loads = [
        pltpu.make_async_copy(live_hbm, live_ref, load_sem.at[5]),
        pltpu.make_async_copy(c_hbm, cv, load_sem.at[0]),
        pltpu.make_async_copy(a_hbm.at[:rim], av.at[:rim], load_sem.at[1]),
        pltpu.make_async_copy(a_hbm.at[voxels:], av.at[voxels:], load_sem.at[2]),
        pltpu.make_async_copy(y_hbm, yv, load_sem.at[3]),
        pltpu.make_async_copy(a_hbm.at[rim:voxels], av.at[rim:voxels], load_sem.at[4]),
    ]
    barrier = pltpu.get_barrier_semaphore()

    def greet(**device):
        pl.semaphore_signal(barrier, inc=1, device_id=device, device_id_type=MESH)

    half = parts // 2
    across = t + 1 - 2 * lax.rem(t, 2)
    along = [lax.rem(t + 2 * k, parts) for k in range(1, half)]
    beyond = [across] + [lax.rem(across + 2 * k, parts) for k in range(1, half)]

    @pl.when(has_next)
    def _():
        greet(slab=s + 1)

    @pl.when(has_prev)
    def _():
        greet(slab=s - 1)

    @pl.when(jnp.logical_not(patient))
    def _():
        for to in along:
            greet(tm=to)

    @pl.when(early)
    def _():
        for to in beyond:
            greet(tm=to)

    @pl.when(early & has_prev)
    def _():
        greet(slab=s - 1, tm=t * 0 + parts - 1)

    @pl.when(first & has_prev)
    def _():
        for i in range(1, parts - 1):
            greet(slab=s - 1, tm=t + i)

    for load in loads:
        load.start()

    rim_copy = remote(y_hbm.at[:, :rim], rim_in, (h_ss, h_rs), (0, 0), slab=s - 1)
    head_copy = remote(head_out, head_in, (h_ss, h_rs), (1, 1), slab=s - 1)
    tail_copy = remote(tail_out, tail_in, (h_ss, h_rs), (2, 2), slab=s + 1)

    for load in loads[:5]:
        load.wait()
    live = lax.broadcasted_iota(jnp.int32, (1, neurons), 1) < live_ref[s]
    keep_tail = jnp.where(has_next, 1.0, 0.0).astype(F32)
    start = jnp.where(live, cv[...], 0.0)
    c_high, c_low = halves(start)
    head = av[:rim]
    tail = (av[voxels:].astype(F32) * keep_tail).astype(BF16)
    av[voxels:] = tail
    head_out[...] = dot(c_high, head, 1, 1) + dot(c_low, head, 1, 1) - yv[:, :rim].astype(F32)
    tail_out[...] = dot(c_high, tail, 1, 1) + dot(c_low, tail, 1, 1)

    y_copies = []

    def pack(p, span):
        base = p * share - p * share // 128 * 128
        for k in range(wide // 128):
            y_send[p, k * frames : (k + 1) * frames] = span[:, base + k * 128 : base + (k + 1) * 128]

    def pack_rest(p, columns):
        pair = jnp.concatenate([columns[: rest // 2], columns[rest // 2 :]], 1)
        y_send[p, wide // 128 * frames :] = pair.astype(BF16)

    group = lax.broadcasted_iota(jnp.int32, (1, 128), 1) // rest
    left = jnp.zeros((frames, 128), F32)
    for p in range(parts - 1):
        tile0 = p * share // 128
        pack(p, yv[:, tile0 * 128 : (tile0 + 3) * 128])
        left = jnp.where(group == p, yv[:, (tile0 + 2) * 128 : (tile0 + 3) * 128].astype(F32), left)
    left_t = left.T
    for p in range(parts - 1):
        pack_rest(p, left_t[p * rest : (p + 1) * rest])

    def count(condition, amount=1):
        return jnp.where(condition, jnp.int32(amount), jnp.int32(0))

    heard = count(has_next) + count(has_prev) + count(late, half) + count(jnp.logical_not(patient), half - 1)
    heard = heard + count(has_next & jnp.logical_not(first)) + count(last & has_next, half - 1)
    pl.semaphore_wait(barrier, heard)

    @pl.when(has_prev)
    def _():
        head_copy.start()

    @pl.when(has_next)
    def _():
        tail_copy.start()

    @pl.when(has_prev)
    def _():
        rim_copy.start()

    @pl.when(late)
    def _():
        for to in beyond:
            pl.semaphore_signal(ready, inc=1, device_id={"tm": to}, device_id_type=MESH)

    @pl.when(last & has_next)
    def _():
        for i in range(1, parts, 2):
            pl.semaphore_signal(
                side_ready, inc=1, device_id={"slab": s + 1, "tm": t - i}, device_id_type=MESH
            )

    routes = list(enumerate(beyond, half)) + list(enumerate(along, 1))
    for i, to in routes:
        copy = remote(y_send.at[to], y_recv.at[i], (y_ss, y_rs), (i, i), tm=to)
        y_copies.append((i, to, copy))

    def send_shares(stage):
        for i, to, copy in y_copies:
            crossing = i >= half
            if crossing:
                due = jnp.int32(LATE_CROSS[0][i - half])
                for zone, stages in enumerate(LATE_CROSS):
                    due = jnp.where(s * len(LATE_CROSS) // slabs == zone, stages[i - half], due)
                due = jnp.where(late, jnp.where(to == 0, 0, due), EARLY_CROSS)
            else:
                due = jnp.where(patient, 3, jnp.where(late, 2, 0))
            due = jnp.where(to == parts - 1, jnp.maximum(due, 2), due)

            @pl.when(due == stage)
            def _(copy=copy):
                copy.start()

    send_shares(0)

    loads[5].wait()
    foot = av[...]
    gram = dot(foot, foot, 0, 0)
    eye = lax.broadcasted_iota(jnp.int32, (neurons, neurons), 0) == lax.broadcasted_iota(
        jnp.int32, (neurons, neurons), 1
    )
    scale = jnp.sum(jnp.where(eye, gram, 0.0), 0, keepdims=True) + 1e-6
    own_drive = dot(yv[...], av[:voxels])
    coupled = dot(start, gram, precision=lax.Precision.HIGHEST)
    base = own_drive - coupled

    @pl.when(has_next)
    def _():
        head_copy.wait_recv()

    @pl.when(has_prev)
    def _():
        tail_copy.wait_recv()

    @pl.when(jnp.logical_not(has_next))
    def _():
        head_in[...] = jnp.zeros_like(head_in)

    @pl.when(jnp.logical_not(has_prev))
    def _():
        tail_in[...] = jnp.zeros_like(tail_in)

    nh, nl = halves(head_in[...])
    ph, pw = halves(tail_in[...])
    outside = dot(
        jnp.concatenate([nh, nl, ph, pw], 1), jnp.concatenate([tail, tail, head, head], 0)
    )
    base = base - outside
    done = []
    for g in range(neurons // GROUP):
        cut = slice(g * GROUP, (g + 1) * GROUP)
        change = base[:, cut]
        for h in range(g):
            moved = done[h] - start[:, h * GROUP : (h + 1) * GROUP]
            change = change - dot(
                moved, gram[h * GROUP : (h + 1) * GROUP, cut], precision=lax.Precision.HIGHEST
            )
        done.append(
            jnp.where(
                live[:, cut], jnp.maximum(start[:, cut] + change / scale[:, cut], 0.0), 0.0
            )
        )
    new_tr = jnp.concatenate(done, 1)
    rounded = new_tr.astype(BF16)
    b_all[0] = rounded

    b_cross = remote(b_all.at[0], b_all.at[half], (b_ss, b_rs), (half, half), tm=across)

    @pl.when(late)
    def _():
        b_cross.start()

    def slot_at(x_to, z_to):
        away = lax.rem(x_to - t // 2 + parts, half)
        return jnp.where(lax.rem(t, 2) == z_to, away, half + away)

    to_first = slot_at(0, 0)
    tail_side = remote(
        side_tail, side_out.at[to_first], (s_ss, s_rs), (0, to_first), slab=s + 1, tm=t * 0
    )
    to_last = slot_at(half - 1, 1)
    head_side = remote(
        side_head.at[0], side_out.at[to_last], (s_ss, s_rs), (1, to_last), slab=s - 1, tm=t * 0 + parts - 1
    )
    late_side = remote(
        side_head.at[pl.ds(1, half)], side_out.at[pl.ds(0, half)], (s_ss, s_rs), (2, parts), slab=s - 1
    )
    side_tail[...] = dot(rounded, tail, 1, 1).astype(BF16)

    @pl.when(has_next)
    def _():
        tail_side.start()

    b_copies = []
    for k, to in enumerate(along, 1):
        copy = remote(b_all.at[0], b_all.at[k], (b_ss, b_rs), (k, k), tm=to)
        b_copies.append(copy)

    @pl.when(jnp.logical_not(patient))
    def _():
        for copy in b_copies:
            copy.start()

    @pl.when(has_next)
    def _():
        rim_copy.wait_recv()

    @pl.when(jnp.logical_not(has_next))
    def _():
        rim_in[...] = jnp.zeros_like(rim_in)

    rim_y = rim_in[...]
    p = parts - 1
    tile0 = p * share // 128
    span = jnp.concatenate([yv[:, tile0 * 128 :], rim_y], 1)
    pack(p, span)
    pack_rest(p, rim_y.astype(F32).T[p * rest :])
    @pl.when(early)
    def _():
        pl.semaphore_wait(ready, half)
        b_cross.start()

    send_shares(2)
    tr_out[...] = new_tr

    @pl.when(jnp.logical_not(last & has_prev))
    def _():
        side_head[0] = dot(rounded, head, 1, 1).astype(BF16)

    b_cross.wait_recv()

    @pl.when(patient)
    def _():
        for copy in b_copies:
            copy.start()

    passed = []
    for k, to in enumerate(along, 1):
        copy = remote(b_all.at[half], b_all.at[half + k], (b_ss, b_rs), (half + k, half + k), tm=to)
        copy.start()
        passed.append(copy)

    @pl.when(early & has_prev)
    def _():
        pl.semaphore_wait(side_ready, 1)
        head_side.start()

    send_shares(3)

    @pl.when(last & has_prev)
    def _():
        for copy in b_copies:
            copy.wait_recv()
        odd = b_all[:half].reshape(half * frames, neurons)
        side_head[1:] = dot(odd, av[:rim], 1, 1).astype(BF16).reshape(half, frames, rim)
        late_side.start()

    row0 = pl.multiple_of(t * share, 16)
    row = row0 + lax.broadcasted_iota(jnp.int32, (share, 1), 0)
    mine = av[pl.ds(row0, share)].astype(F32)
    share_out[...] = jnp.where(live & (row < rows), mine, 0.0).astype(BF16)

    per = wide // 128

    def voxels_first(base):
        tiles = [
            y_recv[base : base + half, k * frames : (k + 1) * frames].reshape(half * frames, 128).T
            for k in range(per)
        ]
        pairs = [y_recv[base + i, per * frames :].astype(F32) for i in range(half)]
        low = jnp.concatenate([q[:, :frames] for q in pairs], 1)
        high = jnp.concatenate([q[:, frames:] for q in pairs], 1)
        return jnp.concatenate(tiles + [jnp.concatenate([low, high], 0).astype(BF16)], 0)

    y_recv[0] = y_send[t]
    for i, _, copy in y_copies:
        if i < half:
            copy.wait_recv()

    @pl.when(jnp.logical_not(last & has_prev))
    def _():
        for copy in b_copies:
            copy.wait_recv()

    near = b_all[:half].reshape(half * frames, neurons)
    q_part[...] = dot(near, near, 0, 0)
    m_part[...] = dot(voxels_first(0), near)

    @pl.when(first & has_prev)
    def _():
        for i in range(half):
            remote(side_tail, side_out.at[i], (s_ss, s_rs), (0, i), slab=s).wait_recv()
        sides = side_out[:half].reshape(half * frames, rim)
        m_part[:rim] = m_part[:rim] - dot(sides, near, 0, 0)

    @pl.when(last & has_next)
    def _():
        late_side.wait_recv()
        sides = side_out[:half].reshape(half * frames, rim)
        m_part[share - rim :] = m_part[share - rim :] - dot(sides, near, 0, 0)

    for i, _, copy in y_copies:
        if i >= half:
            copy.wait_recv()
    yt_out[...] = voxels_first(half)
    for copy in passed:
        copy.wait_recv()

    @pl.when((first & has_prev) | (last & has_next))
    def _():
        for i in range(half, parts):
            remote(side_tail, side_out.at[i], (s_ss, s_rs), (0, i), slab=s).wait_recv()

    for _, _, copy in y_copies:
        copy.wait_send()
    b_cross.wait_send()
    for copy in b_copies + passed:
        copy.wait_send()

    @pl.when(has_prev)
    def _():
        rim_copy.wait_send()
        head_copy.wait_send()

    @pl.when(early & has_prev)
    def _():
        head_side.wait_send()

    @pl.when(last & has_prev)
    def _():
        late_side.wait_send()

    @pl.when(has_next)
    def _():
        tail_copy.wait_send()
        tail_side.wait_send()


def update_kernel(dims, tr, b_all, yt, side, mine, q_part, m_part, tr_hbm, foot_hbm, delta, foot, sems):
    slabs, parts, frames, voxels, rows, neurons = dims
    rim = rows - voxels
    share = rows // parts
    half = parts // 2
    s = lax.axis_index("slab")
    t = lax.axis_index("tm")
    stores = [pltpu.make_async_copy(tr, tr_hbm, sems.at[0])]
    stores[0].start()
    far = b_all[half:].reshape(half * frames, neurons)
    q = q_part[...] + dot(far, far, 0, 0)
    delta[...] = m_part[...] + dot(yt[...], far)

    @pl.when((t == 0) & (s > 0))
    def _():
        delta[:rim] = delta[:rim] - dot(side[half:].reshape(half * frames, rim), far, 0, 0)

    @pl.when((t == parts - 1) & (s < slabs - 1))
    def _():
        delta[share - rim :] = delta[share - rim :] - dot(
            side[half:].reshape(half * frames, rim), far, 0, 0
        )

    eye = lax.broadcasted_iota(jnp.int32, (neurons, neurons), 0) == lax.broadcasted_iota(
        jnp.int32, (neurons, neurons), 1
    )
    scale = jnp.maximum(jnp.sum(jnp.where(eye, q, 0.0), 0, keepdims=True), 1.0)
    q_high, q_low = halves(q)
    cut = share // 32 * 16
    for n, span in enumerate((slice(0, cut), slice(cut, share))):
        base = mine[span]
        coupling = dot(base, q_high) + dot(base, q_low)
        foot[span] = jnp.maximum(
            base.astype(F32) + (delta[span] - coupling) / scale, 0.0
        ).astype(BF16)
        store = pltpu.make_async_copy(foot.at[span], foot_hbm.at[span], sems.at[1 + n])
        store.start()
        stores.append(store)
    for store in stores:
        store.wait()


def solution(mesh):
    slabs, parts = mesh.shape["slab"], mesh.shape["tm"]

    def on_device(recording, footprints, traces, live_count):
        frames, voxels = recording.shape
        rows, neurons = footprints.shape
        rim = rows - voxels
        share = rows // parts
        half = parts // 2
        dims = (slabs, parts, frames, voxels, rows, neurons)
        hbm = pl.BlockSpec(memory_space=pltpu.HBM)
        vmem = pl.BlockSpec(memory_space=pltpu.VMEM)
        packed = share // 128 * frames + share % 128 // 2
        dma = pltpu.SemaphoreType.DMA
        tr, b_all, yt, side, mine, q_part, m_part = pl.pallas_call(
            functools.partial(exchange_kernel, dims),
            out_shape=[
                pltpu.VMEM((frames, neurons), F32),
                pltpu.VMEM((parts, frames, neurons), BF16),
                pltpu.VMEM((share, half * frames), BF16),
                pltpu.VMEM((parts, frames, rim), BF16),
                pltpu.VMEM((share, neurons), BF16),
                pltpu.VMEM((neurons, neurons), F32),
                pltpu.VMEM((share, neurons), F32),
            ],
            in_specs=[hbm, hbm, hbm, hbm],
            out_specs=[vmem] * 7,
            scratch_shapes=[
                pltpu.SMEM((slabs,), jnp.int32),
                pltpu.VMEM((frames, voxels), BF16),
                pltpu.VMEM((rows, neurons), BF16),
                pltpu.VMEM((frames, neurons), F32),
                pltpu.VMEM((parts, packed, 128), BF16),
                pltpu.VMEM((parts, packed, 128), BF16),
                pltpu.VMEM((frames, rim), BF16),
                pltpu.VMEM((frames, rim), F32),
                pltpu.VMEM((frames, rim), F32),
                pltpu.VMEM((frames, rim), F32),
                pltpu.VMEM((frames, rim), F32),
                pltpu.VMEM((half + 1, frames, rim), BF16),
                pltpu.VMEM((frames, rim), BF16),
                dma((6,)),
                dma((parts,)),
                dma((parts,)),
                dma((parts,)),
                dma((parts,)),
                dma((3,)),
                dma((3,)),
                dma((3,)),
                dma((parts + 1,)),
                pltpu.SemaphoreType.REGULAR,
                pltpu.SemaphoreType.REGULAR,
            ],
            compiler_params=pltpu.CompilerParams(
                collective_id=0, has_side_effects=True, vmem_limit_bytes=60 * 2**20
            ),
            name="exchange",
        )(live_count, recording, footprints, traces)
        return pl.pallas_call(
            functools.partial(update_kernel, dims),
            out_shape=[
                jax.ShapeDtypeStruct((frames, neurons), F32),
                jax.ShapeDtypeStruct((share, neurons), BF16),
            ],
            in_specs=[vmem] * 7,
            out_specs=[hbm, hbm],
            scratch_shapes=[
                pltpu.VMEM((share, neurons), F32),
                pltpu.VMEM((share, neurons), BF16),
                dma((3,)),
            ],
            compiler_params=pltpu.CompilerParams(vmem_limit_bytes=32 * 2**20),
            name="update",
        )(tr, b_all, yt, side, mine, q_part, m_part)

    placed = (P("tm", "slab"), P(None, "slab"), P("tm", "slab"), P())
    return jax.shard_map(
        on_device,
        mesh=mesh,
        in_specs=placed,
        out_specs=(P("tm", "slab"), P("tm", "slab")),
        check_vma=False,
    )
```

```python
import functools

import jax
import jax.numpy as jnp
from jax import lax
from jax.experimental import pallas as pl
from jax.experimental.pallas import tpu as pltpu
from jax.sharding import PartitionSpec as P

MESH = pl.DeviceIdType.MESH
F32 = jnp.float32
BF16 = jnp.bfloat16
GROUP = 128
LATE_CROSS = ((0, 0, 2, 2), (0, 0, 0, 2), (0, 0, 0, 2), (0, 2, 2, 2))
EARLY_CROSS = 2
PATIENT = 2


def dot(a, b, ca=1, cb=0, precision=None):
    return lax.dot_general(
        a, b, (((ca,), (cb,)), ((), ())), preferred_element_type=F32, precision=precision
    )


def halves(x):
    high = x.astype(BF16)
    return high, (x - high.astype(F32)).astype(BF16)


def remote(src, dst, sems, index, **device):
    return pltpu.make_async_remote_copy(
        src_ref=src,
        dst_ref=dst,
        send_sem=sems[0].at[index[0]],
        recv_sem=sems[1].at[index[1]],
        device_id=device,
        device_id_type=MESH,
    )


def exchange_kernel(
    dims,
    live_hbm, y_hbm, a_hbm, c_hbm,
    tr_out, b_all, yt_out, side_out, share_out, q_part, m_part,
    live_ref, yv, av, cv, y_send, y_recv, rim_in, head_out, tail_out, head_in, tail_in,
    side_head, side_tail,
    load_sem, y_ss, y_rs, b_ss, b_rs, h_ss, h_rs, s_ss, s_rs, ready, side_ready,
):
    slabs, parts, frames, voxels, rows, neurons = dims
    rim = rows - voxels
    share = rows // parts
    wide = share // 128 * 128
    rest = share - wide
    s = lax.axis_index("slab")
    t = lax.axis_index("tm")
    has_next = s < slabs - 1
    has_prev = s > 0
    first, last = t == 0, t == parts - 1
    early = lax.rem(t, 2) == 0
    late = jnp.logical_not(early)
    patient = late & (s * len(LATE_CROSS) // slabs < PATIENT)

    loads = [
        pltpu.make_async_copy(live_hbm, live_ref, load_sem.at[5]),
        pltpu.make_async_copy(c_hbm, cv, load_sem.at[0]),
        pltpu.make_async_copy(a_hbm.at[:rim], av.at[:rim], load_sem.at[1]),
        pltpu.make_async_copy(a_hbm.at[voxels:], av.at[voxels:], load_sem.at[2]),
        pltpu.make_async_copy(y_hbm, yv, load_sem.at[3]),
        pltpu.make_async_copy(a_hbm.at[rim:voxels], av.at[rim:voxels], load_sem.at[4]),
    ]
    barrier = pltpu.get_barrier_semaphore()

    def greet(**device):
        pl.semaphore_signal(barrier, inc=1, device_id=device, device_id_type=MESH)

    half = parts // 2
    across = t + 1 - 2 * lax.rem(t, 2)
    along = [lax.rem(t + 2 * k, parts) for k in range(1, half)]
    beyond = [across] + [lax.rem(across + 2 * k, parts) for k in range(1, half)]

    @pl.when(has_next)
    def _():
        greet(slab=s + 1)

    @pl.when(has_prev)
    def _():
        greet(slab=s - 1)

    @pl.when(jnp.logical_not(patient))
    def _():
        for to in along:
            greet(tm=to)

    @pl.when(early)
    def _():
        for to in beyond:
            greet(tm=to)

    @pl.when(early & has_prev)
    def _():
        greet(slab=s - 1, tm=t * 0 + parts - 1)

    @pl.when(first & has_prev)
    def _():
        for i in range(1, parts - 1):
            greet(slab=s - 1, tm=t + i)

    for load in loads:
        load.start()

    rim_copy = remote(y_hbm.at[:, :rim], rim_in, (h_ss, h_rs), (0, 0), slab=s - 1)
    head_copy = remote(head_out, head_in, (h_ss, h_rs), (1, 1), slab=s - 1)
    tail_copy = remote(tail_out, tail_in, (h_ss, h_rs), (2, 2), slab=s + 1)

    for load in loads[:5]:
        load.wait()
    live = lax.broadcasted_iota(jnp.int32, (1, neurons), 1) < live_ref[s]
    keep_tail = jnp.where(has_next, 1.0, 0.0).astype(F32)
    start = jnp.where(live, cv[...], 0.0)
    c_high, c_low = halves(start)
    head = av[:rim]
    tail = (av[voxels:].astype(F32) * keep_tail).astype(BF16)
    av[voxels:] = tail
    head_out[...] = dot(c_high, head, 1, 1) + dot(c_low, head, 1, 1) - yv[:, :rim].astype(F32)
    tail_out[...] = dot(c_high, tail, 1, 1) + dot(c_low, tail, 1, 1)

    y_copies = []

    def pack(p, span):
        base = p * share - p * share // 128 * 128
        for k in range(wide // 128):
            y_send[p, k * frames : (k + 1) * frames] = span[:, base + k * 128 : base + (k + 1) * 128]

    def pack_rest(p, columns):
        pair = jnp.concatenate([columns[: rest // 2], columns[rest // 2 :]], 1)
        y_send[p, wide // 128 * frames :] = pair.astype(BF16)

    group = lax.broadcasted_iota(jnp.int32, (1, 128), 1) // rest
    left = jnp.zeros((frames, 128), F32)
    for p in range(parts - 1):
        tile0 = p * share // 128
        pack(p, yv[:, tile0 * 128 : (tile0 + 3) * 128])
        left = jnp.where(group == p, yv[:, (tile0 + 2) * 128 : (tile0 + 3) * 128].astype(F32), left)
    left_t = left.T
    for p in range(parts - 1):
        pack_rest(p, left_t[p * rest : (p + 1) * rest])

    def count(condition, amount=1):
        return jnp.where(condition, jnp.int32(amount), jnp.int32(0))

    heard = count(has_next) + count(has_prev) + count(late, half) + count(jnp.logical_not(patient), half - 1)
    heard = heard + count(has_next & jnp.logical_not(first)) + count(last & has_next, half - 1)
    pl.semaphore_wait(barrier, heard)

    @pl.when(has_prev)
    def _():
        head_copy.start()

    @pl.when(has_next)
    def _():
        tail_copy.start()

    @pl.when(has_prev)
    def _():
        rim_copy.start()

    @pl.when(late)
    def _():
        for to in beyond:
            pl.semaphore_signal(ready, inc=1, device_id={"tm": to}, device_id_type=MESH)

    @pl.when(last & has_next)
    def _():
        for i in range(1, parts, 2):
            pl.semaphore_signal(
                side_ready, inc=1, device_id={"slab": s + 1, "tm": t - i}, device_id_type=MESH
            )

    routes = list(enumerate(beyond, half)) + list(enumerate(along, 1))
    for i, to in routes:
        copy = remote(y_send.at[to], y_recv.at[i], (y_ss, y_rs), (i, i), tm=to)
        y_copies.append((i, to, copy))

    def send_shares(stage):
        for i, to, copy in y_copies:
            crossing = i >= half
            if crossing:
                due = jnp.int32(LATE_CROSS[0][i - half])
                for zone, stages in enumerate(LATE_CROSS):
                    due = jnp.where(s * len(LATE_CROSS) // slabs == zone, stages[i - half], due)
                due = jnp.where(late, jnp.where(to == 0, 0, due), EARLY_CROSS)
            else:
                due = jnp.where(patient, 3, jnp.where(late, 2, 0))
            due = jnp.where(to == parts - 1, jnp.maximum(due, 2), due)

            @pl.when(due == stage)
            def _(copy=copy):
                copy.start()

    send_shares(0)

    loads[5].wait()
    foot = av[...]
    gram = dot(foot, foot, 0, 0)
    eye = lax.broadcasted_iota(jnp.int32, (neurons, neurons), 0) == lax.broadcasted_iota(
        jnp.int32, (neurons, neurons), 1
    )
    scale = jnp.sum(jnp.where(eye, gram, 0.0), 0, keepdims=True) + 1e-6
    own_drive = dot(yv[...], av[:voxels])
    coupled = dot(start, gram, precision=lax.Precision.HIGHEST)
    base = own_drive - coupled

    @pl.when(has_next)
    def _():
        head_copy.wait_recv()

    @pl.when(has_prev)
    def _():
        tail_copy.wait_recv()

    @pl.when(jnp.logical_not(has_next))
    def _():
        head_in[...] = jnp.zeros_like(head_in)

    @pl.when(jnp.logical_not(has_prev))
    def _():
        tail_in[...] = jnp.zeros_like(tail_in)

    nh, nl = halves(head_in[...])
    ph, pw = halves(tail_in[...])
    outside = dot(
        jnp.concatenate([nh, nl, ph, pw], 1), jnp.concatenate([tail, tail, head, head], 0)
    )
    base = base - outside
    done = []
    for g in range(neurons // GROUP):
        cut = slice(g * GROUP, (g + 1) * GROUP)
        change = base[:, cut]
        for h in range(g):
            moved = done[h] - start[:, h * GROUP : (h + 1) * GROUP]
            change = change - dot(
                moved, gram[h * GROUP : (h + 1) * GROUP, cut], precision=lax.Precision.HIGHEST
            )
        done.append(
            jnp.where(
                live[:, cut], jnp.maximum(start[:, cut] + change / scale[:, cut], 0.0), 0.0
            )
        )
    new_tr = jnp.concatenate(done, 1)
    rounded = new_tr.astype(BF16)
    b_all[0] = rounded

    b_cross = remote(b_all.at[0], b_all.at[half], (b_ss, b_rs), (half, half), tm=across)

    @pl.when(late)
    def _():
        b_cross.start()

    def slot_at(x_to, z_to):
        away = lax.rem(x_to - t // 2 + parts, half)
        return jnp.where(lax.rem(t, 2) == z_to, away, half + away)

    to_first = slot_at(0, 0)
    tail_side = remote(
        side_tail, side_out.at[to_first], (s_ss, s_rs), (0, to_first), slab=s + 1, tm=t * 0
    )
    to_last = slot_at(half - 1, 1)
    head_side = remote(
        side_head.at[0], side_out.at[to_last], (s_ss, s_rs), (1, to_last), slab=s - 1, tm=t * 0 + parts - 1
    )
    late_side = remote(
        side_head.at[pl.ds(1, half)], side_out.at[pl.ds(0, half)], (s_ss, s_rs), (2, parts), slab=s - 1
    )
    side_tail[...] = dot(rounded, tail, 1, 1).astype(BF16)

    @pl.when(has_next)
    def _():
        tail_side.start()

    b_copies = []
    for k, to in enumerate(along, 1):
        copy = remote(b_all.at[0], b_all.at[k], (b_ss, b_rs), (k, k), tm=to)
        b_copies.append(copy)

    @pl.when(jnp.logical_not(patient))
    def _():
        for copy in b_copies:
            copy.start()

    @pl.when(has_next)
    def _():
        rim_copy.wait_recv()

    @pl.when(jnp.logical_not(has_next))
    def _():
        rim_in[...] = jnp.zeros_like(rim_in)

    rim_y = rim_in[...]
    p = parts - 1
    tile0 = p * share // 128
    span = jnp.concatenate([yv[:, tile0 * 128 :], rim_y], 1)
    pack(p, span)
    pack_rest(p, rim_y.astype(F32).T[p * rest :])
    @pl.when(early)
    def _():
        pl.semaphore_wait(ready, half)
        b_cross.start()

    send_shares(2)
    tr_out[...] = new_tr

    @pl.when(jnp.logical_not(last & has_prev))
    def _():
        side_head[0] = dot(rounded, head, 1, 1).astype(BF16)

    b_cross.wait_recv()

    @pl.when(patient)
    def _():
        for copy in b_copies:
            copy.start()

    passed = []
    for k, to in enumerate(along, 1):
        copy = remote(b_all.at[half], b_all.at[half + k], (b_ss, b_rs), (half + k, half + k), tm=to)
        copy.start()
        passed.append(copy)

    @pl.when(early & has_prev)
    def _():
        pl.semaphore_wait(side_ready, 1)
        head_side.start()

    send_shares(3)

    @pl.when(last & has_prev)
    def _():
        for copy in b_copies:
            copy.wait_recv()
        odd = b_all[:half].reshape(half * frames, neurons)
        side_head[1:] = dot(odd, av[:rim], 1, 1).astype(BF16).reshape(half, frames, rim)
        late_side.start()

    row0 = pl.multiple_of(t * share, 16)
    row = row0 + lax.broadcasted_iota(jnp.int32, (share, 1), 0)
    mine = av[pl.ds(row0, share)].astype(F32)
    share_out[...] = jnp.where(live & (row < rows), mine, 0.0).astype(BF16)

    per = wide // 128

    def voxels_first(base, many):
        tiles = [
            y_recv[base : base + many, k * frames : (k + 1) * frames].reshape(many * frames, 128).T
            for k in range(per)
        ]
        pairs = [y_recv[base + i, per * frames :].astype(F32) for i in range(many)]
        low = jnp.concatenate([q[:, :frames] for q in pairs], 1)
        high = jnp.concatenate([q[:, frames:] for q in pairs], 1)
        return jnp.concatenate(tiles + [jnp.concatenate([low, high], 0).astype(BF16)], 0)

    y_recv[0] = y_send[t]
    for i, _, copy in y_copies:
        if i < half:
            copy.wait_recv()

    @pl.when(jnp.logical_not(last & has_prev))
    def _():
        for copy in b_copies:
            copy.wait_recv()

    near = b_all[:half].reshape(half * frames, neurons)
    q_part[...] = dot(near, near, 0, 0)
    m_part[...] = dot(voxels_first(0, half), near)

    @pl.when(first & has_prev)
    def _():
        for i in range(half):
            remote(side_tail, side_out.at[i], (s_ss, s_rs), (0, i), slab=s).wait_recv()
        sides = side_out[:half].reshape(half * frames, rim)
        m_part[:rim] = m_part[:rim] - dot(sides, near, 0, 0)

    @pl.when(last & has_next)
    def _():
        late_side.wait_recv()
        sides = side_out[:half].reshape(half * frames, rim)
        m_part[share - rim :] = m_part[share - rim :] - dot(sides, near, 0, 0)

    for n in range(0, half, 2):
        for i, _, copy in y_copies:
            if i - half in (n, n + 1):
                copy.wait_recv()
        yt_out[:, n * frames : (n + 2) * frames] = voxels_first(half + n, 2)
    for copy in passed:
        copy.wait_recv()

    @pl.when((first & has_prev) | (last & has_next))
    def _():
        for i in range(half, parts):
            remote(side_tail, side_out.at[i], (s_ss, s_rs), (0, i), slab=s).wait_recv()

    for _, _, copy in y_copies:
        copy.wait_send()
    b_cross.wait_send()
    for copy in b_copies + passed:
        copy.wait_send()

    @pl.when(has_prev)
    def _():
        rim_copy.wait_send()
        head_copy.wait_send()

    @pl.when(early & has_prev)
    def _():
        head_side.wait_send()

    @pl.when(last & has_prev)
    def _():
        late_side.wait_send()

    @pl.when(has_next)
    def _():
        tail_copy.wait_send()
        tail_side.wait_send()


def update_kernel(dims, tr, b_all, yt, side, mine, q_part, m_part, tr_hbm, foot_hbm, foot, sems):
    slabs, parts, frames, voxels, rows, neurons = dims
    rim = rows - voxels
    share = rows // parts
    half = parts // 2
    s = lax.axis_index("slab")
    t = lax.axis_index("tm")
    stores = [pltpu.make_async_copy(tr, tr_hbm, sems.at[0])]
    stores[0].start()
    far = b_all[half:].reshape(half * frames, neurons)
    q = q_part[...] + dot(far, far, 0, 0)
    sides = dot(side[half:].reshape(half * frames, rim), far, 0, 0)
    top = jnp.where((t == 0) & (s > 0), sides, 0.0)
    bottom = jnp.where((t == parts - 1) & (s < slabs - 1), sides, 0.0)
    middle = jnp.zeros((share - 2 * rim, neurons), F32)
    delta = m_part[...] + dot(yt[...], far) - jnp.concatenate([top, middle, bottom], 0)
    eye = lax.broadcasted_iota(jnp.int32, (neurons, neurons), 0) == lax.broadcasted_iota(
        jnp.int32, (neurons, neurons), 1
    )
    scale = jnp.maximum(jnp.sum(jnp.where(eye, q, 0.0), 0, keepdims=True), 1.0)
    q_high, q_low = halves(q)
    cut = share // 32 * 16
    for n, span in enumerate((slice(0, cut), slice(cut, share))):
        base = mine[span]
        coupling = dot(base, q_high) + dot(base, q_low)
        foot[span] = jnp.maximum(
            base.astype(F32) + (delta[span] - coupling) / scale, 0.0
        ).astype(BF16)
        store = pltpu.make_async_copy(foot.at[span], foot_hbm.at[span], sems.at[1 + n])
        store.start()
        stores.append(store)
    for store in stores:
        store.wait()


def solution(mesh):
    slabs, parts = mesh.shape["slab"], mesh.shape["tm"]

    def on_device(recording, footprints, traces, live_count):
        frames, voxels = recording.shape
        rows, neurons = footprints.shape
        rim = rows - voxels
        share = rows // parts
        half = parts // 2
        dims = (slabs, parts, frames, voxels, rows, neurons)
        hbm = pl.BlockSpec(memory_space=pltpu.HBM)
        vmem = pl.BlockSpec(memory_space=pltpu.VMEM)
        packed = share // 128 * frames + share % 128 // 2
        dma = pltpu.SemaphoreType.DMA
        tr, b_all, yt, side, mine, q_part, m_part = pl.pallas_call(
            functools.partial(exchange_kernel, dims),
            out_shape=[
                pltpu.VMEM((frames, neurons), F32),
                pltpu.VMEM((parts, frames, neurons), BF16),
                pltpu.VMEM((share, half * frames), BF16),
                pltpu.VMEM((parts, frames, rim), BF16),
                pltpu.VMEM((share, neurons), BF16),
                pltpu.VMEM((neurons, neurons), F32),
                pltpu.VMEM((share, neurons), F32),
            ],
            in_specs=[hbm, hbm, hbm, hbm],
            out_specs=[vmem] * 7,
            scratch_shapes=[
                pltpu.SMEM((slabs,), jnp.int32),
                pltpu.VMEM((frames, voxels), BF16),
                pltpu.VMEM((rows, neurons), BF16),
                pltpu.VMEM((frames, neurons), F32),
                pltpu.VMEM((parts, packed, 128), BF16),
                pltpu.VMEM((parts, packed, 128), BF16),
                pltpu.VMEM((frames, rim), BF16),
                pltpu.VMEM((frames, rim), F32),
                pltpu.VMEM((frames, rim), F32),
                pltpu.VMEM((frames, rim), F32),
                pltpu.VMEM((frames, rim), F32),
                pltpu.VMEM((half + 1, frames, rim), BF16),
                pltpu.VMEM((frames, rim), BF16),
                dma((6,)),
                dma((parts,)),
                dma((parts,)),
                dma((parts,)),
                dma((parts,)),
                dma((3,)),
                dma((3,)),
                dma((3,)),
                dma((parts + 1,)),
                pltpu.SemaphoreType.REGULAR,
                pltpu.SemaphoreType.REGULAR,
            ],
            compiler_params=pltpu.CompilerParams(
                collective_id=0, has_side_effects=True, vmem_limit_bytes=60 * 2**20
            ),
            name="exchange",
        )(live_count, recording, footprints, traces)
        return pl.pallas_call(
            functools.partial(update_kernel, dims),
            out_shape=[
                jax.ShapeDtypeStruct((frames, neurons), F32),
                jax.ShapeDtypeStruct((share, neurons), BF16),
            ],
            in_specs=[vmem] * 7,
            out_specs=[hbm, hbm],
            scratch_shapes=[
                pltpu.VMEM((share, neurons), BF16),
                dma((3,)),
            ],
            compiler_params=pltpu.CompilerParams(vmem_limit_bytes=32 * 2**20),
            name="update",
        )(tr, b_all, yt, side, mine, q_part, m_part)

    placed = (P("tm", "slab"), P(None, "slab"), P("tm", "slab"), P())
    return jax.shard_map(
        on_device,
        mesh=mesh,
        in_specs=placed,
        out_specs=(P("tm", "slab"), P("tm", "slab")),
        check_vma=False,
    )
```

```python
import functools

import jax
import jax.numpy as jnp
from jax import lax
from jax.experimental import pallas as pl
from jax.experimental.pallas import tpu as pltpu
from jax.sharding import PartitionSpec as P

MESH = pl.DeviceIdType.MESH
F32 = jnp.float32
BF16 = jnp.bfloat16
GROUP = 128
LATE_CROSS = ((0, 0, 2, 2), (0, 0, 0, 2), (0, 0, 0, 2), (0, 2, 2, 2))
EARLY_CROSS = 2
PATIENT = 2
PIECES = 2


def dot(a, b, ca=1, cb=0, precision=None):
    return lax.dot_general(
        a, b, (((ca,), (cb,)), ((), ())), preferred_element_type=F32, precision=precision
    )


def halves(x):
    high = x.astype(BF16)
    return high, (x - high.astype(F32)).astype(BF16)


def remote(src, dst, sems, index, **device):
    return pltpu.make_async_remote_copy(
        src_ref=src,
        dst_ref=dst,
        send_sem=sems[0].at[index[0]],
        recv_sem=sems[1].at[index[1]],
        device_id=device,
        device_id_type=MESH,
    )


def exchange_kernel(
    dims,
    live_hbm, y_hbm, a_hbm, c_hbm,
    tr_out, b_all, yt_out, side_out, share_out, q_part, m_part,
    live_ref, yv, av, cv, y_send, y_recv, rim_in, head_out, tail_out, head_in, tail_in,
    side_head, side_tail,
    load_sem, y_ss, y_rs, b_ss, b_rs, h_ss, h_rs, s_ss, s_rs, ready, side_ready,
):
    slabs, parts, frames, voxels, rows, neurons = dims
    rim = rows - voxels
    share = rows // parts
    wide = share // 128 * 128
    rest = share - wide
    s = lax.axis_index("slab")
    t = lax.axis_index("tm")
    has_next = s < slabs - 1
    has_prev = s > 0
    first, last = t == 0, t == parts - 1
    early = lax.rem(t, 2) == 0
    late = jnp.logical_not(early)
    patient = late & (s * len(LATE_CROSS) // slabs < PATIENT)

    loads = [
        pltpu.make_async_copy(live_hbm, live_ref, load_sem.at[5]),
        pltpu.make_async_copy(c_hbm, cv, load_sem.at[0]),
        pltpu.make_async_copy(a_hbm.at[:rim], av.at[:rim], load_sem.at[1]),
        pltpu.make_async_copy(a_hbm.at[voxels:], av.at[voxels:], load_sem.at[2]),
        pltpu.make_async_copy(y_hbm, yv, load_sem.at[3]),
        pltpu.make_async_copy(a_hbm.at[rim:voxels], av.at[rim:voxels], load_sem.at[4]),
    ]
    barrier = pltpu.get_barrier_semaphore()

    def greet(**device):
        pl.semaphore_signal(barrier, inc=1, device_id=device, device_id_type=MESH)

    half = parts // 2
    across = t + 1 - 2 * lax.rem(t, 2)
    along = [lax.rem(t + 2 * k, parts) for k in range(1, half)]
    beyond = [across] + [lax.rem(across + 2 * k, parts) for k in range(1, half)]

    @pl.when(has_next)
    def _():
        greet(slab=s + 1)

    @pl.when(has_prev)
    def _():
        greet(slab=s - 1)

    @pl.when(jnp.logical_not(patient))
    def _():
        for to in along:
            greet(tm=to)

    @pl.when(early)
    def _():
        for to in beyond:
            greet(tm=to)

    @pl.when(early & has_prev)
    def _():
        greet(slab=s - 1, tm=t * 0 + parts - 1)

    @pl.when(first & has_prev)
    def _():
        for i in range(1, parts - 1):
            greet(slab=s - 1, tm=t + i)

    for load in loads:
        load.start()

    rim_copy = remote(y_hbm.at[:, :rim], rim_in, (h_ss, h_rs), (0, 0), slab=s - 1)
    head_copy = remote(head_out, head_in, (h_ss, h_rs), (1, 1), slab=s - 1)
    tail_copy = remote(tail_out, tail_in, (h_ss, h_rs), (2, 2), slab=s + 1)

    for load in loads[:5]:
        load.wait()
    live = lax.broadcasted_iota(jnp.int32, (1, neurons), 1) < live_ref[s]
    keep_tail = jnp.where(has_next, 1.0, 0.0).astype(F32)
    start = jnp.where(live, cv[...], 0.0)
    c_high, c_low = halves(start)
    head = av[:rim]
    tail = (av[voxels:].astype(F32) * keep_tail).astype(BF16)
    av[voxels:] = tail
    head_out[...] = dot(c_high, head, 1, 1) + dot(c_low, head, 1, 1) - yv[:, :rim].astype(F32)
    tail_out[...] = dot(c_high, tail, 1, 1) + dot(c_low, tail, 1, 1)

    y_copies = []

    def pack(p, span):
        base = p * share - p * share // 128 * 128
        for k in range(wide // 128):
            y_send[p, k * frames : (k + 1) * frames] = span[:, base + k * 128 : base + (k + 1) * 128]

    def pack_rest(p, columns):
        pair = jnp.concatenate([columns[: rest // 2], columns[rest // 2 :]], 1)
        y_send[p, wide // 128 * frames :] = pair.astype(BF16)

    group = lax.broadcasted_iota(jnp.int32, (1, 128), 1) // rest
    left = jnp.zeros((frames, 128), F32)
    for p in range(parts - 1):
        tile0 = p * share // 128
        pack(p, yv[:, tile0 * 128 : (tile0 + 3) * 128])
        left = jnp.where(group == p, yv[:, (tile0 + 2) * 128 : (tile0 + 3) * 128].astype(F32), left)
    left_t = left.T
    for p in range(parts - 1):
        pack_rest(p, left_t[p * rest : (p + 1) * rest])

    def count(condition, amount=1):
        return jnp.where(condition, jnp.int32(amount), jnp.int32(0))

    heard = count(has_next) + count(has_prev) + count(late, half) + count(jnp.logical_not(patient), half - 1)
    heard = heard + count(has_next & jnp.logical_not(first)) + count(last & has_next, half - 1)
    pl.semaphore_wait(barrier, heard)

    @pl.when(has_prev)
    def _():
        head_copy.start()

    @pl.when(has_next)
    def _():
        tail_copy.start()

    @pl.when(has_prev)
    def _():
        rim_copy.start()

    @pl.when(late)
    def _():
        for to in beyond:
            pl.semaphore_signal(ready, inc=1, device_id={"tm": to}, device_id_type=MESH)

    @pl.when(last & has_next)
    def _():
        for i in range(1, parts, 2):
            pl.semaphore_signal(
                side_ready, inc=1, device_id={"slab": s + 1, "tm": t - i}, device_id_type=MESH
            )

    routes = list(enumerate(beyond, half)) + list(enumerate(along, 1))
    for i, to in routes:
        copy = remote(y_send.at[to], y_recv.at[i], (y_ss, y_rs), (i, i), tm=to)
        y_copies.append((i, to, copy))

    def send_shares(stage):
        for i, to, copy in y_copies:
            crossing = i >= half
            if crossing:
                due = jnp.int32(LATE_CROSS[0][i - half])
                for zone, stages in enumerate(LATE_CROSS):
                    due = jnp.where(s * len(LATE_CROSS) // slabs == zone, stages[i - half], due)
                due = jnp.where(late, jnp.where(to == 0, 0, due), EARLY_CROSS)
            else:
                due = jnp.where(patient, 3, jnp.where(late, 2, 0))
            due = jnp.where(to == parts - 1, jnp.maximum(due, 2), due)

            @pl.when(due == stage)
            def _(copy=copy):
                copy.start()

    send_shares(0)

    loads[5].wait()
    foot = av[...]
    gram = dot(foot, foot, 0, 0)
    eye = lax.broadcasted_iota(jnp.int32, (neurons, neurons), 0) == lax.broadcasted_iota(
        jnp.int32, (neurons, neurons), 1
    )
    scale = jnp.sum(jnp.where(eye, gram, 0.0), 0, keepdims=True) + 1e-6
    own_drive = dot(yv[...], av[:voxels])
    coupled = dot(start, gram, precision=lax.Precision.HIGHEST)
    base = own_drive - coupled

    @pl.when(has_next)
    def _():
        head_copy.wait_recv()

    @pl.when(has_prev)
    def _():
        tail_copy.wait_recv()

    @pl.when(jnp.logical_not(has_next))
    def _():
        head_in[...] = jnp.zeros_like(head_in)

    @pl.when(jnp.logical_not(has_prev))
    def _():
        tail_in[...] = jnp.zeros_like(tail_in)

    nh, nl = halves(head_in[...])
    ph, pw = halves(tail_in[...])
    outside = dot(
        jnp.concatenate([nh, nl, ph, pw], 1), jnp.concatenate([tail, tail, head, head], 0)
    )
    base = base - outside
    done = []
    for g in range(neurons // GROUP):
        cut = slice(g * GROUP, (g + 1) * GROUP)
        change = base[:, cut]
        for h in range(g):
            moved = done[h] - start[:, h * GROUP : (h + 1) * GROUP]
            change = change - dot(
                moved, gram[h * GROUP : (h + 1) * GROUP, cut], precision=lax.Precision.HIGHEST
            )
        done.append(
            jnp.where(
                live[:, cut], jnp.maximum(start[:, cut] + change / scale[:, cut], 0.0), 0.0
            )
        )
    new_tr = jnp.concatenate(done, 1)
    rounded = new_tr.astype(BF16)
    b_all[0] = rounded

    pieces = [(n * parts, pl.ds(n * frames // PIECES, frames // PIECES)) for n in range(PIECES)]
    b_cross = [
        remote(b_all.at[0, span], b_all.at[half, span], (b_ss, b_rs), (n + half, n + half), tm=across)
        for n, span in pieces
    ]

    @pl.when(late)
    def _():
        for copy in b_cross:
            copy.start()

    def slot_at(x_to, z_to):
        away = lax.rem(x_to - t // 2 + parts, half)
        return jnp.where(lax.rem(t, 2) == z_to, away, half + away)

    to_first = slot_at(0, 0)
    tail_side = remote(
        side_tail, side_out.at[to_first], (s_ss, s_rs), (0, to_first), slab=s + 1, tm=t * 0
    )
    to_last = slot_at(half - 1, 1)
    head_side = remote(
        side_head.at[0], side_out.at[to_last], (s_ss, s_rs), (1, to_last), slab=s - 1, tm=t * 0 + parts - 1
    )
    late_side = remote(
        side_head.at[pl.ds(1, half)], side_out.at[pl.ds(0, half)], (s_ss, s_rs), (2, parts), slab=s - 1
    )
    side_tail[...] = dot(rounded, tail, 1, 1).astype(BF16)

    @pl.when(has_next)
    def _():
        tail_side.start()

    b_copies = []
    for k, to in enumerate(along, 1):
        copy = remote(b_all.at[0], b_all.at[k], (b_ss, b_rs), (k, k), tm=to)
        b_copies.append(copy)

    @pl.when(jnp.logical_not(patient))
    def _():
        for copy in b_copies:
            copy.start()

    @pl.when(has_next)
    def _():
        rim_copy.wait_recv()

    @pl.when(jnp.logical_not(has_next))
    def _():
        rim_in[...] = jnp.zeros_like(rim_in)

    rim_y = rim_in[...]
    p = parts - 1
    tile0 = p * share // 128
    span = jnp.concatenate([yv[:, tile0 * 128 :], rim_y], 1)
    pack(p, span)
    pack_rest(p, rim_y.astype(F32).T[p * rest :])
    @pl.when(early)
    def _():
        pl.semaphore_wait(ready, half)
        for copy in b_cross:
            copy.start()

    send_shares(2)
    tr_out[...] = new_tr

    @pl.when(jnp.logical_not(last & has_prev))
    def _():
        side_head[0] = dot(rounded, head, 1, 1).astype(BF16)

    passed = []
    for (n, span), crossed in zip(pieces, b_cross):
        crossed.wait_recv()
        if n == 0:

            @pl.when(patient)
            def _():
                for copy in b_copies:
                    copy.start()

        for k, to in enumerate(along, 1):
            slot = half + k
            copy = remote(
                b_all.at[half, span], b_all.at[slot, span], (b_ss, b_rs), (n + slot, n + slot), tm=to
            )
            copy.start()
            passed.append(copy)

    @pl.when(early & has_prev)
    def _():
        pl.semaphore_wait(side_ready, 1)
        head_side.start()

    send_shares(3)

    @pl.when(last & has_prev)
    def _():
        for copy in b_copies:
            copy.wait_recv()
        odd = b_all[:half].reshape(half * frames, neurons)
        side_head[1:] = dot(odd, av[:rim], 1, 1).astype(BF16).reshape(half, frames, rim)
        late_side.start()

    row0 = pl.multiple_of(t * share, 16)
    row = row0 + lax.broadcasted_iota(jnp.int32, (share, 1), 0)
    mine = av[pl.ds(row0, share)].astype(F32)
    share_out[...] = jnp.where(live & (row < rows), mine, 0.0).astype(BF16)

    per = wide // 128

    def voxels_first(base, many):
        tiles = [
            y_recv[base : base + many, k * frames : (k + 1) * frames].reshape(many * frames, 128).T
            for k in range(per)
        ]
        pairs = [y_recv[base + i, per * frames :].astype(F32) for i in range(many)]
        low = jnp.concatenate([q[:, :frames] for q in pairs], 1)
        high = jnp.concatenate([q[:, frames:] for q in pairs], 1)
        return jnp.concatenate(tiles + [jnp.concatenate([low, high], 0).astype(BF16)], 0)

    y_recv[0] = y_send[t]
    for i, _, copy in y_copies:
        if i < half:
            copy.wait_recv()

    @pl.when(jnp.logical_not(last & has_prev))
    def _():
        for copy in b_copies:
            copy.wait_recv()

    near = b_all[:half].reshape(half * frames, neurons)
    q_part[...] = dot(near, near, 0, 0)
    m_part[...] = dot(voxels_first(0, half), near)

    @pl.when(first & has_prev)
    def _():
        for i in range(half):
            remote(side_tail, side_out.at[i], (s_ss, s_rs), (0, i), slab=s).wait_recv()
        sides = side_out[:half].reshape(half * frames, rim)
        m_part[:rim] = m_part[:rim] - dot(sides, near, 0, 0)

    @pl.when(last & has_next)
    def _():
        late_side.wait_recv()
        sides = side_out[:half].reshape(half * frames, rim)
        m_part[share - rim :] = m_part[share - rim :] - dot(sides, near, 0, 0)

    for n in range(0, half, 2):
        for i, _, copy in y_copies:
            if i - half in (n, n + 1):
                copy.wait_recv()
        yt_out[:, n * frames : (n + 2) * frames] = voxels_first(half + n, 2)
    for copy in passed:
        copy.wait_recv()

    @pl.when((first & has_prev) | (last & has_next))
    def _():
        for i in range(half, parts):
            remote(side_tail, side_out.at[i], (s_ss, s_rs), (0, i), slab=s).wait_recv()

    for _, _, copy in y_copies:
        copy.wait_send()
    for copy in b_cross + b_copies + passed:
        copy.wait_send()

    @pl.when(has_prev)
    def _():
        rim_copy.wait_send()
        head_copy.wait_send()

    @pl.when(early & has_prev)
    def _():
        head_side.wait_send()

    @pl.when(last & has_prev)
    def _():
        late_side.wait_send()

    @pl.when(has_next)
    def _():
        tail_copy.wait_send()
        tail_side.wait_send()


def update_kernel(dims, tr, b_all, yt, side, mine, q_part, m_part, tr_hbm, foot_hbm, foot, sems):
    slabs, parts, frames, voxels, rows, neurons = dims
    rim = rows - voxels
    share = rows // parts
    half = parts // 2
    s = lax.axis_index("slab")
    t = lax.axis_index("tm")
    stores = [pltpu.make_async_copy(tr, tr_hbm, sems.at[0])]
    stores[0].start()
    far = b_all[half:].reshape(half * frames, neurons)
    q = q_part[...] + dot(far, far, 0, 0)
    sides = dot(side[half:].reshape(half * frames, rim), far, 0, 0)
    top = jnp.where((t == 0) & (s > 0), sides, 0.0)
    bottom = jnp.where((t == parts - 1) & (s < slabs - 1), sides, 0.0)
    middle = jnp.zeros((share - 2 * rim, neurons), F32)
    delta = m_part[...] + dot(yt[...], far) - jnp.concatenate([top, middle, bottom], 0)
    eye = lax.broadcasted_iota(jnp.int32, (neurons, neurons), 0) == lax.broadcasted_iota(
        jnp.int32, (neurons, neurons), 1
    )
    scale = jnp.maximum(jnp.sum(jnp.where(eye, q, 0.0), 0, keepdims=True), 1.0)
    q_high, q_low = halves(q)
    cut = share // 32 * 16
    for n, span in enumerate((slice(0, cut), slice(cut, share))):
        base = mine[span]
        coupling = dot(base, q_high) + dot(base, q_low)
        foot[span] = jnp.maximum(
            base.astype(F32) + (delta[span] - coupling) / scale, 0.0
        ).astype(BF16)
        store = pltpu.make_async_copy(foot.at[span], foot_hbm.at[span], sems.at[1 + n])
        store.start()
        stores.append(store)
    for store in stores:
        store.wait()


def solution(mesh):
    slabs, parts = mesh.shape["slab"], mesh.shape["tm"]

    def on_device(recording, footprints, traces, live_count):
        frames, voxels = recording.shape
        rows, neurons = footprints.shape
        rim = rows - voxels
        share = rows // parts
        half = parts // 2
        dims = (slabs, parts, frames, voxels, rows, neurons)
        hbm = pl.BlockSpec(memory_space=pltpu.HBM)
        vmem = pl.BlockSpec(memory_space=pltpu.VMEM)
        packed = share // 128 * frames + share % 128 // 2
        dma = pltpu.SemaphoreType.DMA
        tr, b_all, yt, side, mine, q_part, m_part = pl.pallas_call(
            functools.partial(exchange_kernel, dims),
            out_shape=[
                pltpu.VMEM((frames, neurons), F32),
                pltpu.VMEM((parts, frames, neurons), BF16),
                pltpu.VMEM((share, half * frames), BF16),
                pltpu.VMEM((parts, frames, rim), BF16),
                pltpu.VMEM((share, neurons), BF16),
                pltpu.VMEM((neurons, neurons), F32),
                pltpu.VMEM((share, neurons), F32),
            ],
            in_specs=[hbm, hbm, hbm, hbm],
            out_specs=[vmem] * 7,
            scratch_shapes=[
                pltpu.SMEM((slabs,), jnp.int32),
                pltpu.VMEM((frames, voxels), BF16),
                pltpu.VMEM((rows, neurons), BF16),
                pltpu.VMEM((frames, neurons), F32),
                pltpu.VMEM((parts, packed, 128), BF16),
                pltpu.VMEM((parts, packed, 128), BF16),
                pltpu.VMEM((frames, rim), BF16),
                pltpu.VMEM((frames, rim), F32),
                pltpu.VMEM((frames, rim), F32),
                pltpu.VMEM((frames, rim), F32),
                pltpu.VMEM((frames, rim), F32),
                pltpu.VMEM((half + 1, frames, rim), BF16),
                pltpu.VMEM((frames, rim), BF16),
                dma((6,)),
                dma((parts,)),
                dma((parts,)),
                dma((PIECES * parts,)),
                dma((PIECES * parts,)),
                dma((3,)),
                dma((3,)),
                dma((3,)),
                dma((parts + 1,)),
                pltpu.SemaphoreType.REGULAR,
                pltpu.SemaphoreType.REGULAR,
            ],
            compiler_params=pltpu.CompilerParams(
                collective_id=0, has_side_effects=True, vmem_limit_bytes=60 * 2**20
            ),
            name="exchange",
        )(live_count, recording, footprints, traces)
        return pl.pallas_call(
            functools.partial(update_kernel, dims),
            out_shape=[
                jax.ShapeDtypeStruct((frames, neurons), F32),
                jax.ShapeDtypeStruct((share, neurons), BF16),
            ],
            in_specs=[vmem] * 7,
            out_specs=[hbm, hbm],
            scratch_shapes=[
                pltpu.VMEM((share, neurons), BF16),
                dma((3,)),
            ],
            compiler_params=pltpu.CompilerParams(vmem_limit_bytes=32 * 2**20),
            name="update",
        )(tr, b_all, yt, side, mine, q_part, m_part)

    placed = (P("tm", "slab"), P(None, "slab"), P("tm", "slab"), P())
    return jax.shard_map(
        on_device,
        mesh=mesh,
        in_specs=placed,
        out_specs=(P("tm", "slab"), P("tm", "slab")),
        check_vma=False,
    )
```

```python
import functools

import jax
import jax.numpy as jnp
from jax import lax
from jax.experimental import pallas as pl
from jax.experimental.pallas import tpu as pltpu
from jax.sharding import PartitionSpec as P

MESH = pl.DeviceIdType.MESH
F32 = jnp.float32
BF16 = jnp.bfloat16
GROUP = 128
LATE_CROSS = ((0, 2, 2, 2), (0, 0, 0, 2), (0, 0, 2, 2), (0, 2, 2, 2))
EARLY_CROSS = 2
PATIENT = 2
PIECES = 2


def dot(a, b, ca=1, cb=0, precision=None):
    return lax.dot_general(
        a, b, (((ca,), (cb,)), ((), ())), preferred_element_type=F32, precision=precision
    )


def halves(x):
    high = x.astype(BF16)
    return high, (x - high.astype(F32)).astype(BF16)


def remote(src, dst, sems, index, **device):
    return pltpu.make_async_remote_copy(
        src_ref=src,
        dst_ref=dst,
        send_sem=sems[0].at[index[0]],
        recv_sem=sems[1].at[index[1]],
        device_id=device,
        device_id_type=MESH,
    )


def exchange_kernel(
    dims,
    live_hbm, y_hbm, a_hbm, c_hbm,
    tr_out, b_all, yt_out, side_out, share_out, q_part, m_part,
    live_ref, yv, av, cv, y_send, y_recv, rim_in, head_out, tail_out, head_in, tail_in,
    side_head, side_tail,
    load_sem, y_ss, y_rs, b_ss, b_rs, h_ss, h_rs, s_ss, s_rs, ready, side_ready,
):
    slabs, parts, frames, voxels, rows, neurons = dims
    rim = rows - voxels
    share = rows // parts
    wide = share // 128 * 128
    rest = share - wide
    s = lax.axis_index("slab")
    t = lax.axis_index("tm")
    has_next = s < slabs - 1
    has_prev = s > 0
    first, last = t == 0, t == parts - 1
    early = lax.rem(t, 2) == 0
    late = jnp.logical_not(early)
    patient = late & (s * len(LATE_CROSS) // slabs < PATIENT)

    loads = [
        pltpu.make_async_copy(live_hbm, live_ref, load_sem.at[5]),
        pltpu.make_async_copy(c_hbm, cv, load_sem.at[0]),
        pltpu.make_async_copy(a_hbm.at[:rim], av.at[:rim], load_sem.at[1]),
        pltpu.make_async_copy(a_hbm.at[voxels:], av.at[voxels:], load_sem.at[2]),
        pltpu.make_async_copy(y_hbm, yv, load_sem.at[3]),
        pltpu.make_async_copy(a_hbm.at[rim:voxels], av.at[rim:voxels], load_sem.at[4]),
    ]
    barrier = pltpu.get_barrier_semaphore()

    def greet(**device):
        pl.semaphore_signal(barrier, inc=1, device_id=device, device_id_type=MESH)

    half = parts // 2
    across = t + 1 - 2 * lax.rem(t, 2)
    along = [lax.rem(t + 2 * k, parts) for k in range(1, half)]
    beyond = [across] + [lax.rem(across + 2 * k, parts) for k in range(1, half)]

    @pl.when(has_next)
    def _():
        greet(slab=s + 1)

    @pl.when(has_prev)
    def _():
        greet(slab=s - 1)

    @pl.when(jnp.logical_not(patient))
    def _():
        for to in along:
            greet(tm=to)

    @pl.when(early)
    def _():
        for to in beyond:
            greet(tm=to)

    @pl.when(early & has_prev)
    def _():
        greet(slab=s - 1, tm=t * 0 + parts - 1)

    @pl.when(first & has_prev)
    def _():
        for i in range(1, parts - 1):
            greet(slab=s - 1, tm=t + i)

    for load in loads:
        load.start()

    rim_copy = remote(y_hbm.at[:, :rim], rim_in, (h_ss, h_rs), (0, 0), slab=s - 1)
    head_copy = remote(head_out, head_in, (h_ss, h_rs), (1, 1), slab=s - 1)
    tail_copy = remote(tail_out, tail_in, (h_ss, h_rs), (2, 2), slab=s + 1)

    for load in loads[:5]:
        load.wait()
    live = lax.broadcasted_iota(jnp.int32, (1, neurons), 1) < live_ref[s]
    keep_tail = jnp.where(has_next, 1.0, 0.0).astype(F32)
    start = jnp.where(live, cv[...], 0.0)
    c_high, c_low = halves(start)
    head = av[:rim]
    tail = (av[voxels:].astype(F32) * keep_tail).astype(BF16)
    av[voxels:] = tail
    head_out[...] = dot(c_high, head, 1, 1) + dot(c_low, head, 1, 1) - yv[:, :rim].astype(F32)
    tail_out[...] = dot(c_high, tail, 1, 1) + dot(c_low, tail, 1, 1)

    y_copies = []

    def pack(p, span):
        base = p * share - p * share // 128 * 128
        for k in range(wide // 128):
            y_send[p, k * frames : (k + 1) * frames] = span[:, base + k * 128 : base + (k + 1) * 128]

    def pack_rest(p, columns):
        pair = jnp.concatenate([columns[: rest // 2], columns[rest // 2 :]], 1)
        y_send[p, wide // 128 * frames :] = pair.astype(BF16)

    group = lax.broadcasted_iota(jnp.int32, (1, 128), 1) // rest
    left = jnp.zeros((frames, 128), F32)
    for p in range(parts - 1):
        tile0 = p * share // 128
        pack(p, yv[:, tile0 * 128 : (tile0 + 3) * 128])
        left = jnp.where(group == p, yv[:, (tile0 + 2) * 128 : (tile0 + 3) * 128].astype(F32), left)
    left_t = left.T
    for p in range(parts - 1):
        pack_rest(p, left_t[p * rest : (p + 1) * rest])

    def count(condition, amount=1):
        return jnp.where(condition, jnp.int32(amount), jnp.int32(0))

    heard = count(has_next) + count(has_prev) + count(late, half) + count(jnp.logical_not(patient), half - 1)
    heard = heard + count(has_next & jnp.logical_not(first)) + count(last & has_next, half - 1)
    pl.semaphore_wait(barrier, heard)

    @pl.when(has_prev)
    def _():
        head_copy.start()

    @pl.when(has_next)
    def _():
        tail_copy.start()

    @pl.when(has_prev)
    def _():
        rim_copy.start()

    @pl.when(late)
    def _():
        for to in beyond:
            pl.semaphore_signal(ready, inc=1, device_id={"tm": to}, device_id_type=MESH)

    @pl.when(last & has_next)
    def _():
        for i in range(1, parts, 2):
            pl.semaphore_signal(
                side_ready, inc=1, device_id={"slab": s + 1, "tm": t - i}, device_id_type=MESH
            )

    routes = list(enumerate(beyond, half)) + list(enumerate(along, 1))
    for i, to in routes:
        copy = remote(y_send.at[to], y_recv.at[i], (y_ss, y_rs), (i, i), tm=to)
        y_copies.append((i, to, copy))

    def send_shares(stage):
        for i, to, copy in y_copies:
            crossing = i >= half
            if crossing:
                due = jnp.int32(LATE_CROSS[0][i - half])
                for zone, stages in enumerate(LATE_CROSS):
                    due = jnp.where(s * len(LATE_CROSS) // slabs == zone, stages[i - half], due)
                due = jnp.where(late, jnp.where(to == 0, 0, due), EARLY_CROSS)
            else:
                due = jnp.where(patient, 3, jnp.where(late, 2, 0))
            due = jnp.where(to == parts - 1, jnp.maximum(due, 2), due)

            @pl.when(due == stage)
            def _(copy=copy):
                copy.start()

    send_shares(0)

    loads[5].wait()
    foot = av[...]
    gram = dot(foot, foot, 0, 0)
    eye = lax.broadcasted_iota(jnp.int32, (neurons, neurons), 0) == lax.broadcasted_iota(
        jnp.int32, (neurons, neurons), 1
    )
    scale = jnp.sum(jnp.where(eye, gram, 0.0), 0, keepdims=True) + 1e-6
    own_drive = dot(yv[...], av[:voxels])
    coupled = dot(start, gram, precision=lax.Precision.HIGHEST)
    base = own_drive - coupled

    @pl.when(has_next)
    def _():
        head_copy.wait_recv()

    @pl.when(has_prev)
    def _():
        tail_copy.wait_recv()

    @pl.when(jnp.logical_not(has_next))
    def _():
        head_in[...] = jnp.zeros_like(head_in)

    @pl.when(jnp.logical_not(has_prev))
    def _():
        tail_in[...] = jnp.zeros_like(tail_in)

    nh, nl = halves(head_in[...])
    ph, pw = halves(tail_in[...])
    outside = dot(
        jnp.concatenate([nh, nl, ph, pw], 1), jnp.concatenate([tail, tail, head, head], 0)
    )
    base = base - outside
    done = []
    for g in range(neurons // GROUP):
        cut = slice(g * GROUP, (g + 1) * GROUP)
        change = base[:, cut]
        for h in range(g):
            moved = done[h] - start[:, h * GROUP : (h + 1) * GROUP]
            change = change - dot(
                moved, gram[h * GROUP : (h + 1) * GROUP, cut], precision=lax.Precision.HIGHEST
            )
        done.append(
            jnp.where(
                live[:, cut], jnp.maximum(start[:, cut] + change / scale[:, cut], 0.0), 0.0
            )
        )
    new_tr = jnp.concatenate(done, 1)
    rounded = new_tr.astype(BF16)
    b_all[0] = rounded

    pieces = [(n * parts, pl.ds(n * frames // PIECES, frames // PIECES)) for n in range(PIECES)]
    b_cross = [
        remote(b_all.at[0, span], b_all.at[half, span], (b_ss, b_rs), (n + half, n + half), tm=across)
        for n, span in pieces
    ]

    @pl.when(late)
    def _():
        for copy in b_cross:
            copy.start()

    def slot_at(x_to, z_to):
        away = lax.rem(x_to - t // 2 + parts, half)
        return jnp.where(lax.rem(t, 2) == z_to, away, half + away)

    to_first = slot_at(0, 0)
    tail_side = remote(
        side_tail, side_out.at[to_first], (s_ss, s_rs), (0, to_first), slab=s + 1, tm=t * 0
    )
    to_last = slot_at(half - 1, 1)
    head_side = remote(
        side_head.at[0], side_out.at[to_last], (s_ss, s_rs), (1, to_last), slab=s - 1, tm=t * 0 + parts - 1
    )
    late_side = remote(
        side_head.at[pl.ds(1, half)], side_out.at[pl.ds(0, half)], (s_ss, s_rs), (2, parts), slab=s - 1
    )
    side_tail[...] = dot(rounded, tail, 1, 1).astype(BF16)

    @pl.when(has_next)
    def _():
        tail_side.start()

    b_copies = []
    for k, to in enumerate(along, 1):
        copy = remote(b_all.at[0], b_all.at[k], (b_ss, b_rs), (k, k), tm=to)
        b_copies.append(copy)

    @pl.when(jnp.logical_not(patient))
    def _():
        for copy in b_copies:
            copy.start()

    @pl.when(has_next)
    def _():
        rim_copy.wait_recv()

    @pl.when(jnp.logical_not(has_next))
    def _():
        rim_in[...] = jnp.zeros_like(rim_in)

    rim_y = rim_in[...]
    p = parts - 1
    tile0 = p * share // 128
    span = jnp.concatenate([yv[:, tile0 * 128 :], rim_y], 1)
    pack(p, span)
    pack_rest(p, rim_y.astype(F32).T[p * rest :])
    @pl.when(early)
    def _():
        pl.semaphore_wait(ready, half)
        for copy in b_cross:
            copy.start()

    send_shares(2)
    tr_out[...] = new_tr

    @pl.when(jnp.logical_not(last & has_prev))
    def _():
        side_head[0] = dot(rounded, head, 1, 1).astype(BF16)

    passed = []
    for (n, span), crossed in zip(pieces, b_cross):
        crossed.wait_recv()
        if n == 0:

            @pl.when(patient)
            def _():
                for copy in b_copies:
                    copy.start()

        for k, to in enumerate(along, 1):
            slot = half + k
            copy = remote(
                b_all.at[half, span], b_all.at[slot, span], (b_ss, b_rs), (n + slot, n + slot), tm=to
            )
            copy.start()
            passed.append(copy)

    @pl.when(early & has_prev)
    def _():
        pl.semaphore_wait(side_ready, 1)
        head_side.start()

    send_shares(3)

    @pl.when(last & has_prev)
    def _():
        for copy in b_copies:
            copy.wait_recv()
        odd = b_all[:half].reshape(half * frames, neurons)
        side_head[1:] = dot(odd, av[:rim], 1, 1).astype(BF16).reshape(half, frames, rim)
        late_side.start()

    row0 = pl.multiple_of(t * share, 16)
    row = row0 + lax.broadcasted_iota(jnp.int32, (share, 1), 0)
    mine = av[pl.ds(row0, share)].astype(F32)
    share_out[...] = jnp.where(live & (row < rows), mine, 0.0).astype(BF16)

    per = wide // 128

    def voxels_first(base, many):
        tiles = [
            y_recv[base : base + many, k * frames : (k + 1) * frames].reshape(many * frames, 128).T
            for k in range(per)
        ]
        pairs = [y_recv[base + i, per * frames :].astype(F32) for i in range(many)]
        low = jnp.concatenate([q[:, :frames] for q in pairs], 1)
        high = jnp.concatenate([q[:, frames:] for q in pairs], 1)
        return jnp.concatenate(tiles + [jnp.concatenate([low, high], 0).astype(BF16)], 0)

    y_recv[0] = y_send[t]
    for i, _, copy in y_copies:
        if i < half:
            copy.wait_recv()

    @pl.when(jnp.logical_not(last & has_prev))
    def _():
        for copy in b_copies:
            copy.wait_recv()

    near = b_all[:half].reshape(half * frames, neurons)
    q_part[...] = dot(near, near, 0, 0)
    m_part[...] = dot(voxels_first(0, half), near)

    @pl.when(first & has_prev)
    def _():
        for i in range(half):
            remote(side_tail, side_out.at[i], (s_ss, s_rs), (0, i), slab=s).wait_recv()
        sides = side_out[:half].reshape(half * frames, rim)
        m_part[:rim] = m_part[:rim] - dot(sides, near, 0, 0)

    @pl.when(last & has_next)
    def _():
        late_side.wait_recv()
        sides = side_out[:half].reshape(half * frames, rim)
        m_part[share - rim :] = m_part[share - rim :] - dot(sides, near, 0, 0)

    for n in range(0, half, 2):
        for i, _, copy in y_copies:
            if i - half in (n, n + 1):
                copy.wait_recv()
        yt_out[:, n * frames : (n + 2) * frames] = voxels_first(half + n, 2)
    for copy in passed:
        copy.wait_recv()

    @pl.when((first & has_prev) | (last & has_next))
    def _():
        for i in range(half, parts):
            remote(side_tail, side_out.at[i], (s_ss, s_rs), (0, i), slab=s).wait_recv()

    for _, _, copy in y_copies:
        copy.wait_send()
    for copy in b_cross + b_copies + passed:
        copy.wait_send()

    @pl.when(has_prev)
    def _():
        rim_copy.wait_send()
        head_copy.wait_send()

    @pl.when(early & has_prev)
    def _():
        head_side.wait_send()

    @pl.when(last & has_prev)
    def _():
        late_side.wait_send()

    @pl.when(has_next)
    def _():
        tail_copy.wait_send()
        tail_side.wait_send()


def update_kernel(dims, tr, b_all, yt, side, mine, q_part, m_part, tr_hbm, foot_hbm, foot, sems):
    slabs, parts, frames, voxels, rows, neurons = dims
    rim = rows - voxels
    share = rows // parts
    half = parts // 2
    s = lax.axis_index("slab")
    t = lax.axis_index("tm")
    stores = [pltpu.make_async_copy(tr, tr_hbm, sems.at[0])]
    stores[0].start()
    far = b_all[half:].reshape(half * frames, neurons)
    q = q_part[...] + dot(far, far, 0, 0)
    sides = dot(side[half:].reshape(half * frames, rim), far, 0, 0)
    top = jnp.where((t == 0) & (s > 0), sides, 0.0)
    bottom = jnp.where((t == parts - 1) & (s < slabs - 1), sides, 0.0)
    middle = jnp.zeros((share - 2 * rim, neurons), F32)
    delta = m_part[...] + dot(yt[...], far) - jnp.concatenate([top, middle, bottom], 0)
    eye = lax.broadcasted_iota(jnp.int32, (neurons, neurons), 0) == lax.broadcasted_iota(
        jnp.int32, (neurons, neurons), 1
    )
    scale = jnp.maximum(jnp.sum(jnp.where(eye, q, 0.0), 0, keepdims=True), 1.0)
    q_high, q_low = halves(q)
    cut = share // 32 * 16
    for n, span in enumerate((slice(0, cut), slice(cut, share))):
        base = mine[span]
        coupling = dot(base, q_high) + dot(base, q_low)
        foot[span] = jnp.maximum(
            base.astype(F32) + (delta[span] - coupling) / scale, 0.0
        ).astype(BF16)
        store = pltpu.make_async_copy(foot.at[span], foot_hbm.at[span], sems.at[1 + n])
        store.start()
        stores.append(store)
    for store in stores:
        store.wait()


def solution(mesh):
    slabs, parts = mesh.shape["slab"], mesh.shape["tm"]

    def on_device(recording, footprints, traces, live_count):
        frames, voxels = recording.shape
        rows, neurons = footprints.shape
        rim = rows - voxels
        share = rows // parts
        half = parts // 2
        dims = (slabs, parts, frames, voxels, rows, neurons)
        hbm = pl.BlockSpec(memory_space=pltpu.HBM)
        vmem = pl.BlockSpec(memory_space=pltpu.VMEM)
        packed = share // 128 * frames + share % 128 // 2
        dma = pltpu.SemaphoreType.DMA
        tr, b_all, yt, side, mine, q_part, m_part = pl.pallas_call(
            functools.partial(exchange_kernel, dims),
            out_shape=[
                pltpu.VMEM((frames, neurons), F32),
                pltpu.VMEM((parts, frames, neurons), BF16),
                pltpu.VMEM((share, half * frames), BF16),
                pltpu.VMEM((parts, frames, rim), BF16),
                pltpu.VMEM((share, neurons), BF16),
                pltpu.VMEM((neurons, neurons), F32),
                pltpu.VMEM((share, neurons), F32),
            ],
            in_specs=[hbm, hbm, hbm, hbm],
            out_specs=[vmem] * 7,
            scratch_shapes=[
                pltpu.SMEM((slabs,), jnp.int32),
                pltpu.VMEM((frames, voxels), BF16),
                pltpu.VMEM((rows, neurons), BF16),
                pltpu.VMEM((frames, neurons), F32),
                pltpu.VMEM((parts, packed, 128), BF16),
                pltpu.VMEM((parts, packed, 128), BF16),
                pltpu.VMEM((frames, rim), BF16),
                pltpu.VMEM((frames, rim), F32),
                pltpu.VMEM((frames, rim), F32),
                pltpu.VMEM((frames, rim), F32),
                pltpu.VMEM((frames, rim), F32),
                pltpu.VMEM((half + 1, frames, rim), BF16),
                pltpu.VMEM((frames, rim), BF16),
                dma((6,)),
                dma((parts,)),
                dma((parts,)),
                dma((PIECES * parts,)),
                dma((PIECES * parts,)),
                dma((3,)),
                dma((3,)),
                dma((3,)),
                dma((parts + 1,)),
                pltpu.SemaphoreType.REGULAR,
                pltpu.SemaphoreType.REGULAR,
            ],
            compiler_params=pltpu.CompilerParams(
                collective_id=0, has_side_effects=True, vmem_limit_bytes=60 * 2**20
            ),
            name="exchange",
        )(live_count, recording, footprints, traces)
        return pl.pallas_call(
            functools.partial(update_kernel, dims),
            out_shape=[
                jax.ShapeDtypeStruct((frames, neurons), F32),
                jax.ShapeDtypeStruct((share, neurons), BF16),
            ],
            in_specs=[vmem] * 7,
            out_specs=[hbm, hbm],
            scratch_shapes=[
                pltpu.VMEM((share, neurons), BF16),
                dma((3,)),
            ],
            compiler_params=pltpu.CompilerParams(vmem_limit_bytes=32 * 2**20),
            name="update",
        )(tr, b_all, yt, side, mine, q_part, m_part)

    placed = (P("tm", "slab"), P(None, "slab"), P("tm", "slab"), P())
    return jax.shard_map(
        on_device,
        mesh=mesh,
        in_specs=placed,
        out_specs=(P("tm", "slab"), P("tm", "slab")),
        check_vma=False,
    )
```

```python
import functools

import jax
import jax.numpy as jnp
from jax import lax
from jax.experimental import pallas as pl
from jax.experimental.pallas import tpu as pltpu
from jax.sharding import PartitionSpec as P

MESH = pl.DeviceIdType.MESH
F32 = jnp.float32
BF16 = jnp.bfloat16
GROUP = 128
LATE_CROSS = ((0, 0, 2, 2), (0, 0, 0, 2), (0, 0, 0, 2), (0, 2, 2, 2))
EARLY_CROSS = 2
PATIENT = 2
PIECES = 2


def dot(a, b, ca=1, cb=0, precision=None):
    return lax.dot_general(
        a, b, (((ca,), (cb,)), ((), ())), preferred_element_type=F32, precision=precision
    )


def halves(x):
    high = x.astype(BF16)
    return high, (x - high.astype(F32)).astype(BF16)


def remote(src, dst, sems, index, **device):
    return pltpu.make_async_remote_copy(
        src_ref=src,
        dst_ref=dst,
        send_sem=sems[0].at[index[0]],
        recv_sem=sems[1].at[index[1]],
        device_id=device,
        device_id_type=MESH,
    )


def exchange_kernel(
    dims,
    live_hbm, y_hbm, a_hbm, c_hbm,
    tr_out, b_all, yt_out, side_out, share_out, q_part, m_part,
    live_ref, yv, av, cv, y_send, y_recv, rim_in, head_out, tail_out, head_in, tail_in,
    side_head, side_tail,
    load_sem, y_ss, y_rs, b_ss, b_rs, h_ss, h_rs, s_ss, s_rs, ready, side_ready,
):
    slabs, parts, frames, voxels, rows, neurons = dims
    rim = rows - voxels
    share = rows // parts
    wide = share // 128 * 128
    rest = share - wide
    s = lax.axis_index("slab")
    t = lax.axis_index("tm")
    has_next = s < slabs - 1
    has_prev = s > 0
    first, last = t == 0, t == parts - 1
    early = lax.rem(t, 2) == 0
    late = jnp.logical_not(early)
    patient = late & (s * len(LATE_CROSS) // slabs < PATIENT)

    loads = [
        pltpu.make_async_copy(live_hbm, live_ref, load_sem.at[5]),
        pltpu.make_async_copy(c_hbm, cv, load_sem.at[0]),
        pltpu.make_async_copy(a_hbm.at[:rim], av.at[:rim], load_sem.at[1]),
        pltpu.make_async_copy(a_hbm.at[voxels:], av.at[voxels:], load_sem.at[2]),
        pltpu.make_async_copy(y_hbm, yv, load_sem.at[3]),
        pltpu.make_async_copy(a_hbm.at[rim:voxels], av.at[rim:voxels], load_sem.at[4]),
    ]
    barrier = pltpu.get_barrier_semaphore()

    def greet(**device):
        pl.semaphore_signal(barrier, inc=1, device_id=device, device_id_type=MESH)

    half = parts // 2
    across = t + 1 - 2 * lax.rem(t, 2)
    along = [lax.rem(t + 2 * k, parts) for k in range(1, half)]
    beyond = [across] + [lax.rem(across + 2 * k, parts) for k in range(1, half)]

    @pl.when(has_next)
    def _():
        greet(slab=s + 1)

    @pl.when(has_prev)
    def _():
        greet(slab=s - 1)

    @pl.when(jnp.logical_not(patient))
    def _():
        for to in along:
            greet(tm=to)

    @pl.when(early)
    def _():
        for to in beyond:
            greet(tm=to)

    @pl.when(early & has_prev)
    def _():
        greet(slab=s - 1, tm=t * 0 + parts - 1)

    @pl.when(first & has_prev)
    def _():
        for i in range(1, parts - 1):
            greet(slab=s - 1, tm=t + i)

    for load in loads:
        load.start()

    rim_copy = remote(y_hbm.at[:, :rim], rim_in, (h_ss, h_rs), (0, 0), slab=s - 1)
    head_copy = remote(head_out, head_in, (h_ss, h_rs), (1, 1), slab=s - 1)
    tail_copy = remote(tail_out, tail_in, (h_ss, h_rs), (2, 2), slab=s + 1)

    for load in loads[:5]:
        load.wait()
    live = lax.broadcasted_iota(jnp.int32, (1, neurons), 1) < live_ref[s]
    keep_tail = jnp.where(has_next, 1.0, 0.0).astype(F32)
    start = jnp.where(live, cv[...], 0.0)
    c_high, c_low = halves(start)
    head = av[:rim]
    tail = (av[voxels:].astype(F32) * keep_tail).astype(BF16)
    av[voxels:] = tail
    head_out[...] = dot(c_high, head, 1, 1) + dot(c_low, head, 1, 1) - yv[:, :rim].astype(F32)
    tail_out[...] = dot(c_high, tail, 1, 1) + dot(c_low, tail, 1, 1)

    y_copies = []

    def pack(p, span):
        base = p * share - p * share // 128 * 128
        for k in range(wide // 128):
            y_send[p, k * frames : (k + 1) * frames] = span[:, base + k * 128 : base + (k + 1) * 128]

    def pack_rest(p, columns):
        pair = jnp.concatenate([columns[: rest // 2], columns[rest // 2 :]], 1)
        y_send[p, wide // 128 * frames :] = pair.astype(BF16)

    group = lax.broadcasted_iota(jnp.int32, (1, 128), 1) // rest
    left = jnp.zeros((frames, 128), F32)
    for p in range(parts - 1):
        tile0 = p * share // 128
        pack(p, yv[:, tile0 * 128 : (tile0 + 3) * 128])
        left = jnp.where(group == p, yv[:, (tile0 + 2) * 128 : (tile0 + 3) * 128].astype(F32), left)
    left_t = left.T
    for p in range(parts - 1):
        pack_rest(p, left_t[p * rest : (p + 1) * rest])

    def count(condition, amount=1):
        return jnp.where(condition, jnp.int32(amount), jnp.int32(0))

    heard = count(has_next) + count(has_prev) + count(late, half) + count(jnp.logical_not(patient), half - 1)
    heard = heard + count(has_next & jnp.logical_not(first)) + count(last & has_next, half - 1)
    pl.semaphore_wait(barrier, heard)

    @pl.when(has_prev)
    def _():
        head_copy.start()

    @pl.when(has_next)
    def _():
        tail_copy.start()

    @pl.when(has_prev)
    def _():
        rim_copy.start()

    @pl.when(late)
    def _():
        for to in beyond:
            pl.semaphore_signal(ready, inc=1, device_id={"tm": to}, device_id_type=MESH)

    @pl.when(last & has_next)
    def _():
        for i in range(1, parts, 2):
            pl.semaphore_signal(
                side_ready, inc=1, device_id={"slab": s + 1, "tm": t - i}, device_id_type=MESH
            )

    routes = list(enumerate(beyond, half)) + list(enumerate(along, 1))
    for i, to in routes:
        copy = remote(y_send.at[to], y_recv.at[i], (y_ss, y_rs), (i, i), tm=to)
        y_copies.append((i, to, copy))

    def send_shares(stage):
        for i, to, copy in y_copies:
            crossing = i >= half
            if crossing:
                due = jnp.int32(LATE_CROSS[0][i - half])
                for zone, stages in enumerate(LATE_CROSS):
                    due = jnp.where(s * len(LATE_CROSS) // slabs == zone, stages[i - half], due)
                due = jnp.where(late, jnp.where(to == 0, 0, due), EARLY_CROSS)
            else:
                due = jnp.where(patient, 3, jnp.where(late, 2, 0))
            due = jnp.where(to == parts - 1, jnp.maximum(due, 2), due)

            @pl.when(due == stage)
            def _(copy=copy):
                copy.start()

    send_shares(0)

    loads[5].wait()
    foot = av[...]
    gram = dot(foot, foot, 0, 0)
    eye = lax.broadcasted_iota(jnp.int32, (neurons, neurons), 0) == lax.broadcasted_iota(
        jnp.int32, (neurons, neurons), 1
    )
    scale = jnp.sum(jnp.where(eye, gram, 0.0), 0, keepdims=True) + 1e-6
    own_drive = dot(yv[...], av[:voxels])
    coupled = dot(start, gram, precision=lax.Precision.HIGHEST)
    base = own_drive - coupled
    between = {}
    for g in range(neurons // GROUP):
        for h in range(g):
            g_high, g_low = halves(gram[h * GROUP : (h + 1) * GROUP, g * GROUP : (g + 1) * GROUP])
            between[h, g] = jnp.concatenate([g_high, g_high, g_low], 0)

    @pl.when(has_next)
    def _():
        head_copy.wait_recv()

    @pl.when(has_prev)
    def _():
        tail_copy.wait_recv()

    @pl.when(jnp.logical_not(has_next))
    def _():
        head_in[...] = jnp.zeros_like(head_in)

    @pl.when(jnp.logical_not(has_prev))
    def _():
        tail_in[...] = jnp.zeros_like(tail_in)

    nh, nl = halves(head_in[...])
    ph, pw = halves(tail_in[...])
    outside = dot(
        jnp.concatenate([nh, nl, ph, pw], 1), jnp.concatenate([tail, tail, head, head], 0)
    )
    base = base - outside
    done = []
    for g in range(neurons // GROUP):
        cut = slice(g * GROUP, (g + 1) * GROUP)
        change = base[:, cut]
        for h in range(g):
            m_high, m_low = halves(done[h] - start[:, h * GROUP : (h + 1) * GROUP])
            change = change - dot(jnp.concatenate([m_high, m_low, m_high], 1), between[h, g])
        moved = jnp.maximum(start[:, cut] + change / scale[:, cut], 0.0)
        done.append(jnp.where(live[:, cut], moved, 0.0))
    new_tr = jnp.concatenate(done, 1)
    rounded = new_tr.astype(BF16)
    b_all[0] = rounded

    pieces = [(n * parts, pl.ds(n * frames // PIECES, frames // PIECES)) for n in range(PIECES)]
    b_cross = [
        remote(b_all.at[0, span], b_all.at[half, span], (b_ss, b_rs), (n + half, n + half), tm=across)
        for n, span in pieces
    ]

    @pl.when(late)
    def _():
        for copy in b_cross:
            copy.start()

    def slot_at(x_to, z_to):
        away = lax.rem(x_to - t // 2 + parts, half)
        return jnp.where(lax.rem(t, 2) == z_to, away, half + away)

    to_first = slot_at(0, 0)
    tail_side = remote(
        side_tail, side_out.at[to_first], (s_ss, s_rs), (0, to_first), slab=s + 1, tm=t * 0
    )
    to_last = slot_at(half - 1, 1)
    head_side = remote(
        side_head.at[0], side_out.at[to_last], (s_ss, s_rs), (1, to_last), slab=s - 1, tm=t * 0 + parts - 1
    )
    late_side = remote(
        side_head.at[pl.ds(1, half)], side_out.at[pl.ds(0, half)], (s_ss, s_rs), (2, parts), slab=s - 1
    )
    side_tail[...] = dot(rounded, tail, 1, 1).astype(BF16)

    @pl.when(has_next)
    def _():
        tail_side.start()

    b_copies = []
    for k, to in enumerate(along, 1):
        copy = remote(b_all.at[0], b_all.at[k], (b_ss, b_rs), (k, k), tm=to)
        b_copies.append(copy)

    @pl.when(jnp.logical_not(patient))
    def _():
        for copy in b_copies:
            copy.start()

    @pl.when(has_next)
    def _():
        rim_copy.wait_recv()

    @pl.when(jnp.logical_not(has_next))
    def _():
        rim_in[...] = jnp.zeros_like(rim_in)

    rim_y = rim_in[...]
    p = parts - 1
    tile0 = p * share // 128
    span = jnp.concatenate([yv[:, tile0 * 128 :], rim_y], 1)
    pack(p, span)
    pack_rest(p, rim_y.astype(F32).T[p * rest :])
    @pl.when(early)
    def _():
        pl.semaphore_wait(ready, half)
        for copy in b_cross:
            copy.start()

    send_shares(2)
    tr_out[...] = new_tr

    @pl.when(jnp.logical_not(last & has_prev))
    def _():
        side_head[0] = dot(rounded, head, 1, 1).astype(BF16)

    passed = []
    for (n, span), crossed in zip(pieces, b_cross):
        crossed.wait_recv()
        if n == 0:

            @pl.when(patient)
            def _():
                for copy in b_copies:
                    copy.start()

        for k, to in enumerate(along, 1):
            slot = half + k
            copy = remote(
                b_all.at[half, span], b_all.at[slot, span], (b_ss, b_rs), (n + slot, n + slot), tm=to
            )
            copy.start()
            passed.append(copy)

    @pl.when(early & has_prev)
    def _():
        pl.semaphore_wait(side_ready, 1)
        head_side.start()

    send_shares(3)

    @pl.when(last & has_prev)
    def _():
        for copy in b_copies:
            copy.wait_recv()
        odd = b_all[:half].reshape(half * frames, neurons)
        side_head[1:] = dot(odd, av[:rim], 1, 1).astype(BF16).reshape(half, frames, rim)
        late_side.start()

    row0 = pl.multiple_of(t * share, 16)
    row = row0 + lax.broadcasted_iota(jnp.int32, (share, 1), 0)
    mine = av[pl.ds(row0, share)].astype(F32)
    share_out[...] = jnp.where(live & (row < rows), mine, 0.0).astype(BF16)

    per = wide // 128

    def voxels_first(base, many):
        tiles = [
            y_recv[base : base + many, k * frames : (k + 1) * frames].reshape(many * frames, 128).T
            for k in range(per)
        ]
        pairs = [y_recv[base + i, per * frames :].astype(F32) for i in range(many)]
        low = jnp.concatenate([q[:, :frames] for q in pairs], 1)
        high = jnp.concatenate([q[:, frames:] for q in pairs], 1)
        return jnp.concatenate(tiles + [jnp.concatenate([low, high], 0).astype(BF16)], 0)

    y_recv[0] = y_send[t]
    for i, _, copy in y_copies:
        if i < half:
            copy.wait_recv()

    @pl.when(jnp.logical_not(last & has_prev))
    def _():
        for copy in b_copies:
            copy.wait_recv()

    near = b_all[:half].reshape(half * frames, neurons)
    q_part[...] = dot(near, near, 0, 0)
    m_part[...] = dot(voxels_first(0, half), near)

    @pl.when(first & has_prev)
    def _():
        for i in range(half):
            remote(side_tail, side_out.at[i], (s_ss, s_rs), (0, i), slab=s).wait_recv()
        sides = side_out[:half].reshape(half * frames, rim)
        m_part[:rim] = m_part[:rim] - dot(sides, near, 0, 0)

    @pl.when(last & has_next)
    def _():
        late_side.wait_recv()
        sides = side_out[:half].reshape(half * frames, rim)
        m_part[share - rim :] = m_part[share - rim :] - dot(sides, near, 0, 0)

    for n in range(0, half, 2):
        for i, _, copy in y_copies:
            if i - half in (n, n + 1):
                copy.wait_recv()
        yt_out[:, n * frames : (n + 2) * frames] = voxels_first(half + n, 2)
    for copy in passed:
        copy.wait_recv()

    @pl.when((first & has_prev) | (last & has_next))
    def _():
        for i in range(half, parts):
            remote(side_tail, side_out.at[i], (s_ss, s_rs), (0, i), slab=s).wait_recv()

    for _, _, copy in y_copies:
        copy.wait_send()
    for copy in b_cross + b_copies + passed:
        copy.wait_send()

    @pl.when(has_prev)
    def _():
        rim_copy.wait_send()
        head_copy.wait_send()

    @pl.when(early & has_prev)
    def _():
        head_side.wait_send()

    @pl.when(last & has_prev)
    def _():
        late_side.wait_send()

    @pl.when(has_next)
    def _():
        tail_copy.wait_send()
        tail_side.wait_send()


def update_kernel(dims, tr, b_all, yt, side, mine, q_part, m_part, tr_hbm, foot_hbm, foot, sems):
    slabs, parts, frames, voxels, rows, neurons = dims
    rim = rows - voxels
    share = rows // parts
    half = parts // 2
    s = lax.axis_index("slab")
    t = lax.axis_index("tm")
    stores = [pltpu.make_async_copy(tr, tr_hbm, sems.at[0])]
    stores[0].start()
    far = b_all[half:].reshape(half * frames, neurons)
    q = q_part[...] + dot(far, far, 0, 0)
    sides = dot(side[half:].reshape(half * frames, rim), far, 0, 0)
    top = jnp.where((t == 0) & (s > 0), sides, 0.0)
    bottom = jnp.where((t == parts - 1) & (s < slabs - 1), sides, 0.0)
    middle = jnp.zeros((share - 2 * rim, neurons), F32)
    delta = m_part[...] + dot(yt[...], far) - jnp.concatenate([top, middle, bottom], 0)
    eye = lax.broadcasted_iota(jnp.int32, (neurons, neurons), 0) == lax.broadcasted_iota(
        jnp.int32, (neurons, neurons), 1
    )
    scale = jnp.maximum(jnp.sum(jnp.where(eye, q, 0.0), 0, keepdims=True), 1.0)
    q_high, q_low = halves(q)
    cut = share // 32 * 16
    for n, span in enumerate((slice(0, cut), slice(cut, share))):
        base = mine[span]
        coupling = dot(base, q_high) + dot(base, q_low)
        foot[span] = jnp.maximum(
            base.astype(F32) + (delta[span] - coupling) / scale, 0.0
        ).astype(BF16)
        store = pltpu.make_async_copy(foot.at[span], foot_hbm.at[span], sems.at[1 + n])
        store.start()
        stores.append(store)
    for store in stores:
        store.wait()


def solution(mesh):
    slabs, parts = mesh.shape["slab"], mesh.shape["tm"]

    def on_device(recording, footprints, traces, live_count):
        frames, voxels = recording.shape
        rows, neurons = footprints.shape
        rim = rows - voxels
        share = rows // parts
        half = parts // 2
        dims = (slabs, parts, frames, voxels, rows, neurons)
        hbm = pl.BlockSpec(memory_space=pltpu.HBM)
        vmem = pl.BlockSpec(memory_space=pltpu.VMEM)
        packed = share // 128 * frames + share % 128 // 2
        dma = pltpu.SemaphoreType.DMA
        tr, b_all, yt, side, mine, q_part, m_part = pl.pallas_call(
            functools.partial(exchange_kernel, dims),
            out_shape=[
                pltpu.VMEM((frames, neurons), F32),
                pltpu.VMEM((parts, frames, neurons), BF16),
                pltpu.VMEM((share, half * frames), BF16),
                pltpu.VMEM((parts, frames, rim), BF16),
                pltpu.VMEM((share, neurons), BF16),
                pltpu.VMEM((neurons, neurons), F32),
                pltpu.VMEM((share, neurons), F32),
            ],
            in_specs=[hbm, hbm, hbm, hbm],
            out_specs=[vmem] * 7,
            scratch_shapes=[
                pltpu.SMEM((slabs,), jnp.int32),
                pltpu.VMEM((frames, voxels), BF16),
                pltpu.VMEM((rows, neurons), BF16),
                pltpu.VMEM((frames, neurons), F32),
                pltpu.VMEM((parts, packed, 128), BF16),
                pltpu.VMEM((parts, packed, 128), BF16),
                pltpu.VMEM((frames, rim), BF16),
                pltpu.VMEM((frames, rim), F32),
                pltpu.VMEM((frames, rim), F32),
                pltpu.VMEM((frames, rim), F32),
                pltpu.VMEM((frames, rim), F32),
                pltpu.VMEM((half + 1, frames, rim), BF16),
                pltpu.VMEM((frames, rim), BF16),
                dma((6,)),
                dma((parts,)),
                dma((parts,)),
                dma((PIECES * parts,)),
                dma((PIECES * parts,)),
                dma((3,)),
                dma((3,)),
                dma((3,)),
                dma((parts + 1,)),
                pltpu.SemaphoreType.REGULAR,
                pltpu.SemaphoreType.REGULAR,
            ],
            compiler_params=pltpu.CompilerParams(
                collective_id=0, has_side_effects=True, vmem_limit_bytes=60 * 2**20
            ),
            name="exchange",
        )(live_count, recording, footprints, traces)
        return pl.pallas_call(
            functools.partial(update_kernel, dims),
            out_shape=[
                jax.ShapeDtypeStruct((frames, neurons), F32),
                jax.ShapeDtypeStruct((share, neurons), BF16),
            ],
            in_specs=[vmem] * 7,
            out_specs=[hbm, hbm],
            scratch_shapes=[
                pltpu.VMEM((share, neurons), BF16),
                dma((3,)),
            ],
            compiler_params=pltpu.CompilerParams(vmem_limit_bytes=32 * 2**20),
            name="update",
        )(tr, b_all, yt, side, mine, q_part, m_part)

    placed = (P("tm", "slab"), P(None, "slab"), P("tm", "slab"), P())
    return jax.shard_map(
        on_device,
        mesh=mesh,
        in_specs=placed,
        out_specs=(P("tm", "slab"), P("tm", "slab")),
        check_vma=False,
    )
```

```python
import functools

import jax
import jax.numpy as jnp
from jax import lax
from jax.experimental import pallas as pl
from jax.experimental.pallas import tpu as pltpu
from jax.sharding import PartitionSpec as P

MESH = pl.DeviceIdType.MESH
F32 = jnp.float32
BF16 = jnp.bfloat16
GROUP = 128
LATE_CROSS = ((0, 0, 2, 2), (0, 0, 0, 2), (0, 0, 0, 2), (0, 2, 2, 2))
EARLY_CROSS = 2
PATIENT = 2
PIECES = 2


def dot(a, b, ca=1, cb=0, precision=None):
    return lax.dot_general(
        a, b, (((ca,), (cb,)), ((), ())), preferred_element_type=F32, precision=precision
    )


def halves(x):
    high = x.astype(BF16)
    return high, (x - high.astype(F32)).astype(BF16)


def remote(src, dst, sems, index, **device):
    return pltpu.make_async_remote_copy(
        src_ref=src,
        dst_ref=dst,
        send_sem=sems[0].at[index[0]],
        recv_sem=sems[1].at[index[1]],
        device_id=device,
        device_id_type=MESH,
    )


def exchange_kernel(
    dims,
    live_hbm, y_hbm, a_hbm, c_hbm,
    tr_out, b_all, yt_out, side_out, share_out, q_part, m_part,
    live_ref, yv, av, cv, y_send, y_recv, rim_in, head_out, tail_out, head_in, tail_in,
    side_head, side_tail,
    load_sem, y_ss, y_rs, b_ss, b_rs, h_ss, h_rs, s_ss, s_rs, ready, side_ready,
):
    slabs, parts, frames, voxels, rows, neurons = dims
    rim = rows - voxels
    share = rows // parts
    wide = share // 128 * 128
    rest = share - wide
    s = lax.axis_index("slab")
    t = lax.axis_index("tm")
    has_next = s < slabs - 1
    has_prev = s > 0
    first, last = t == 0, t == parts - 1
    early = lax.rem(t, 2) == 0
    late = jnp.logical_not(early)
    patient = late & (s * len(LATE_CROSS) // slabs < PATIENT)

    loads = [
        pltpu.make_async_copy(live_hbm, live_ref, load_sem.at[5]),
        pltpu.make_async_copy(c_hbm, cv, load_sem.at[0]),
        pltpu.make_async_copy(a_hbm.at[:rim], av.at[:rim], load_sem.at[1]),
        pltpu.make_async_copy(a_hbm.at[voxels:], av.at[voxels:], load_sem.at[2]),
        pltpu.make_async_copy(y_hbm, yv, load_sem.at[3]),
        pltpu.make_async_copy(a_hbm.at[rim:voxels], av.at[rim:voxels], load_sem.at[4]),
    ]
    barrier = pltpu.get_barrier_semaphore()

    def greet(**device):
        pl.semaphore_signal(barrier, inc=1, device_id=device, device_id_type=MESH)

    half = parts // 2
    across = t + 1 - 2 * lax.rem(t, 2)
    along = [lax.rem(t + 2 * k, parts) for k in range(1, half)]
    beyond = [across] + [lax.rem(across + 2 * k, parts) for k in range(1, half)]

    @pl.when(has_next)
    def _():
        greet(slab=s + 1)

    @pl.when(has_prev)
    def _():
        greet(slab=s - 1)

    @pl.when(jnp.logical_not(patient))
    def _():
        for to in along:
            greet(tm=to)

    @pl.when(early)
    def _():
        for to in beyond:
            greet(tm=to)

    @pl.when(early & has_prev)
    def _():
        greet(slab=s - 1, tm=t * 0 + parts - 1)

    @pl.when(first & has_prev)
    def _():
        for i in range(1, parts - 1):
            greet(slab=s - 1, tm=t + i)

    for load in loads:
        load.start()

    rim_copy = remote(y_hbm.at[:, :rim], rim_in, (h_ss, h_rs), (0, 0), slab=s - 1)
    head_copy = remote(head_out, head_in, (h_ss, h_rs), (1, 1), slab=s - 1)
    tail_copy = remote(tail_out, tail_in, (h_ss, h_rs), (2, 2), slab=s + 1)

    for load in loads[:5]:
        load.wait()
    live = lax.broadcasted_iota(jnp.int32, (1, neurons), 1) < live_ref[s]
    keep_tail = jnp.where(has_next, 1.0, 0.0).astype(F32)
    start = jnp.where(live, cv[...], 0.0)
    c_high, c_low = halves(start)
    head = av[:rim]
    tail = (av[voxels:].astype(F32) * keep_tail).astype(BF16)
    av[voxels:] = tail
    head_out[...] = dot(c_high, head, 1, 1) + dot(c_low, head, 1, 1) - yv[:, :rim].astype(F32)
    tail_out[...] = dot(c_high, tail, 1, 1) + dot(c_low, tail, 1, 1)

    y_copies = []

    def pack(p, span):
        base = p * share - p * share // 128 * 128
        for k in range(wide // 128):
            y_send[p, k * frames : (k + 1) * frames] = span[:, base + k * 128 : base + (k + 1) * 128]

    def pack_rest(p, columns):
        pair = jnp.concatenate([columns[: rest // 2], columns[rest // 2 :]], 1)
        y_send[p, wide // 128 * frames :] = pair.astype(BF16)

    group = lax.broadcasted_iota(jnp.int32, (1, 128), 1) // rest
    left = jnp.zeros((frames, 128), F32)
    for p in range(parts - 1):
        tile0 = p * share // 128
        pack(p, yv[:, tile0 * 128 : (tile0 + 3) * 128])
        left = jnp.where(group == p, yv[:, (tile0 + 2) * 128 : (tile0 + 3) * 128].astype(F32), left)
    left_t = left.T
    for p in range(parts - 1):
        pack_rest(p, left_t[p * rest : (p + 1) * rest])

    def count(condition, amount=1):
        return jnp.where(condition, jnp.int32(amount), jnp.int32(0))

    heard = count(has_next) + count(has_prev) + count(late, half) + count(jnp.logical_not(patient), half - 1)
    heard = heard + count(has_next & jnp.logical_not(first)) + count(last & has_next, half - 1)
    pl.semaphore_wait(barrier, heard)

    @pl.when(has_prev)
    def _():
        head_copy.start()

    @pl.when(has_next)
    def _():
        tail_copy.start()

    @pl.when(has_prev)
    def _():
        rim_copy.start()

    @pl.when(late)
    def _():
        for to in beyond:
            pl.semaphore_signal(ready, inc=1, device_id={"tm": to}, device_id_type=MESH)

    @pl.when(last & has_next)
    def _():
        for i in range(1, parts, 2):
            pl.semaphore_signal(
                side_ready, inc=1, device_id={"slab": s + 1, "tm": t - i}, device_id_type=MESH
            )

    routes = list(enumerate(beyond, half)) + list(enumerate(along, 1))
    for i, to in routes:
        copy = remote(y_send.at[to], y_recv.at[i], (y_ss, y_rs), (i, i), tm=to)
        y_copies.append((i, to, copy))

    def send_shares(stage):
        for i, to, copy in y_copies:
            crossing = i >= half
            if crossing:
                due = jnp.int32(LATE_CROSS[0][i - half])
                for zone, stages in enumerate(LATE_CROSS):
                    due = jnp.where(s * len(LATE_CROSS) // slabs == zone, stages[i - half], due)
                due = jnp.where(late, jnp.where((to == 0) & (s * len(LATE_CROSS) // slabs > 0), 0, due), EARLY_CROSS)
            else:
                due = jnp.where(patient, 3, jnp.where(late, 2, 0))
            due = jnp.where(to == parts - 1, jnp.maximum(due, 2), due)

            @pl.when(due == stage)
            def _(copy=copy):
                copy.start()

    send_shares(0)

    loads[5].wait()
    foot = av[...]
    gram = dot(foot, foot, 0, 0)
    eye = lax.broadcasted_iota(jnp.int32, (neurons, neurons), 0) == lax.broadcasted_iota(
        jnp.int32, (neurons, neurons), 1
    )
    scale = jnp.sum(jnp.where(eye, gram, 0.0), 0, keepdims=True) + 1e-6
    own_drive = dot(yv[...], av[:voxels])
    coupled = dot(start, gram, precision=lax.Precision.HIGHEST)
    base = own_drive - coupled
    between = {}
    for g in range(neurons // GROUP):
        for h in range(g):
            g_high, g_low = halves(gram[h * GROUP : (h + 1) * GROUP, g * GROUP : (g + 1) * GROUP])
            between[h, g] = jnp.concatenate([g_high, g_high, g_low], 0)

    @pl.when(has_next)
    def _():
        head_copy.wait_recv()

    @pl.when(has_prev)
    def _():
        tail_copy.wait_recv()

    @pl.when(jnp.logical_not(has_next))
    def _():
        head_in[...] = jnp.zeros_like(head_in)

    @pl.when(jnp.logical_not(has_prev))
    def _():
        tail_in[...] = jnp.zeros_like(tail_in)

    nh, nl = halves(head_in[...])
    ph, pw = halves(tail_in[...])
    outside = dot(
        jnp.concatenate([nh, nl, ph, pw], 1), jnp.concatenate([tail, tail, head, head], 0)
    )
    base = base - outside
    done = []
    for g in range(neurons // GROUP):
        cut = slice(g * GROUP, (g + 1) * GROUP)
        change = base[:, cut]
        for h in range(g):
            m_high, m_low = halves(done[h] - start[:, h * GROUP : (h + 1) * GROUP])
            change = change - dot(jnp.concatenate([m_high, m_low, m_high], 1), between[h, g])
        moved = jnp.maximum(start[:, cut] + change / scale[:, cut], 0.0)
        done.append(jnp.where(live[:, cut], moved, 0.0))
    new_tr = jnp.concatenate(done, 1)
    rounded = new_tr.astype(BF16)
    b_all[0] = rounded

    pieces = [(n * parts, pl.ds(n * frames // PIECES, frames // PIECES)) for n in range(PIECES)]
    b_cross = [
        remote(b_all.at[0, span], b_all.at[half, span], (b_ss, b_rs), (n + half, n + half), tm=across)
        for n, span in pieces
    ]

    @pl.when(late)
    def _():
        for copy in b_cross:
            copy.start()

    def slot_at(x_to, z_to):
        away = lax.rem(x_to - t // 2 + parts, half)
        return jnp.where(lax.rem(t, 2) == z_to, away, half + away)

    to_first = slot_at(0, 0)
    tail_side = remote(
        side_tail, side_out.at[to_first], (s_ss, s_rs), (0, to_first), slab=s + 1, tm=t * 0
    )
    to_last = slot_at(half - 1, 1)
    head_side = remote(
        side_head.at[0], side_out.at[to_last], (s_ss, s_rs), (1, to_last), slab=s - 1, tm=t * 0 + parts - 1
    )
    late_side = remote(
        side_head.at[pl.ds(1, half)], side_out.at[pl.ds(0, half)], (s_ss, s_rs), (2, parts), slab=s - 1
    )
    side_tail[...] = dot(rounded, tail, 1, 1).astype(BF16)

    @pl.when(has_next)
    def _():
        tail_side.start()

    b_copies = []
    for k, to in enumerate(along, 1):
        copy = remote(b_all.at[0], b_all.at[k], (b_ss, b_rs), (k, k), tm=to)
        b_copies.append(copy)

    @pl.when(jnp.logical_not(patient))
    def _():
        for copy in b_copies:
            copy.start()

    @pl.when(has_next)
    def _():
        rim_copy.wait_recv()

    @pl.when(jnp.logical_not(has_next))
    def _():
        rim_in[...] = jnp.zeros_like(rim_in)

    rim_y = rim_in[...]
    p = parts - 1
    tile0 = p * share // 128
    span = jnp.concatenate([yv[:, tile0 * 128 :], rim_y], 1)
    pack(p, span)
    pack_rest(p, rim_y.astype(F32).T[p * rest :])
    @pl.when(early)
    def _():
        pl.semaphore_wait(ready, half)
        for copy in b_cross:
            copy.start()

    send_shares(2)
    tr_out[...] = new_tr

    @pl.when(jnp.logical_not(last & has_prev))
    def _():
        side_head[0] = dot(rounded, head, 1, 1).astype(BF16)

    passed = []
    for (n, span), crossed in zip(pieces, b_cross):
        crossed.wait_recv()
        if n == 0:

            @pl.when(patient)
            def _():
                for copy in b_copies:
                    copy.start()

        for k, to in enumerate(along, 1):
            slot = half + k
            copy = remote(
                b_all.at[half, span], b_all.at[slot, span], (b_ss, b_rs), (n + slot, n + slot), tm=to
            )
            copy.start()
            passed.append(copy)

    @pl.when(early & has_prev)
    def _():
        pl.semaphore_wait(side_ready, 1)
        head_side.start()

    send_shares(3)

    @pl.when(last & has_prev)
    def _():
        for copy in b_copies:
            copy.wait_recv()
        odd = b_all[:half].reshape(half * frames, neurons)
        side_head[1:] = dot(odd, av[:rim], 1, 1).astype(BF16).reshape(half, frames, rim)
        late_side.start()

    row0 = pl.multiple_of(t * share, 16)
    row = row0 + lax.broadcasted_iota(jnp.int32, (share, 1), 0)
    mine = av[pl.ds(row0, share)].astype(F32)
    share_out[...] = jnp.where(live & (row < rows), mine, 0.0).astype(BF16)

    per = wide // 128

    def voxels_first(base, many):
        tiles = [
            y_recv[base : base + many, k * frames : (k + 1) * frames].reshape(many * frames, 128).T
            for k in range(per)
        ]
        pairs = [y_recv[base + i, per * frames :].astype(F32) for i in range(many)]
        low = jnp.concatenate([q[:, :frames] for q in pairs], 1)
        high = jnp.concatenate([q[:, frames:] for q in pairs], 1)
        return jnp.concatenate(tiles + [jnp.concatenate([low, high], 0).astype(BF16)], 0)

    y_recv[0] = y_send[t]
    for i, _, copy in y_copies:
        if i < half:
            copy.wait_recv()

    @pl.when(jnp.logical_not(last & has_prev))
    def _():
        for copy in b_copies:
            copy.wait_recv()

    near = b_all[:half].reshape(half * frames, neurons)
    q_part[...] = dot(near, near, 0, 0)
    m_part[...] = dot(voxels_first(0, half), near)

    @pl.when(first & has_prev)
    def _():
        for i in range(half):
            remote(side_tail, side_out.at[i], (s_ss, s_rs), (0, i), slab=s).wait_recv()
        sides = side_out[:half].reshape(half * frames, rim)
        m_part[:rim] = m_part[:rim] - dot(sides, near, 0, 0)

    @pl.when(last & has_next)
    def _():
        late_side.wait_recv()
        sides = side_out[:half].reshape(half * frames, rim)
        m_part[share - rim :] = m_part[share - rim :] - dot(sides, near, 0, 0)

    for n in range(0, half, 2):
        for i, _, copy in y_copies:
            if i - half in (n, n + 1):
                copy.wait_recv()
        yt_out[:, n * frames : (n + 2) * frames] = voxels_first(half + n, 2)
    for copy in passed:
        copy.wait_recv()

    @pl.when((first & has_prev) | (last & has_next))
    def _():
        for i in range(half, parts):
            remote(side_tail, side_out.at[i], (s_ss, s_rs), (0, i), slab=s).wait_recv()

    for _, _, copy in y_copies:
        copy.wait_send()
    for copy in b_cross + b_copies + passed:
        copy.wait_send()

    @pl.when(has_prev)
    def _():
        rim_copy.wait_send()
        head_copy.wait_send()

    @pl.when(early & has_prev)
    def _():
        head_side.wait_send()

    @pl.when(last & has_prev)
    def _():
        late_side.wait_send()

    @pl.when(has_next)
    def _():
        tail_copy.wait_send()
        tail_side.wait_send()


def update_kernel(dims, tr, b_all, yt, side, mine, q_part, m_part, tr_hbm, foot_hbm, foot, sems):
    slabs, parts, frames, voxels, rows, neurons = dims
    rim = rows - voxels
    share = rows // parts
    half = parts // 2
    s = lax.axis_index("slab")
    t = lax.axis_index("tm")
    stores = [pltpu.make_async_copy(tr, tr_hbm, sems.at[0])]
    stores[0].start()
    far = b_all[half:].reshape(half * frames, neurons)
    q = q_part[...] + dot(far, far, 0, 0)
    sides = dot(side[half:].reshape(half * frames, rim), far, 0, 0)
    top = jnp.where((t == 0) & (s > 0), sides, 0.0)
    bottom = jnp.where((t == parts - 1) & (s < slabs - 1), sides, 0.0)
    middle = jnp.zeros((share - 2 * rim, neurons), F32)
    delta = m_part[...] + dot(yt[...], far) - jnp.concatenate([top, middle, bottom], 0)
    eye = lax.broadcasted_iota(jnp.int32, (neurons, neurons), 0) == lax.broadcasted_iota(
        jnp.int32, (neurons, neurons), 1
    )
    scale = jnp.maximum(jnp.sum(jnp.where(eye, q, 0.0), 0, keepdims=True), 1.0)
    q_high, q_low = halves(q)
    cut = share // 32 * 16
    for n, span in enumerate((slice(0, cut), slice(cut, share))):
        base = mine[span]
        coupling = dot(base, q_high) + dot(base, q_low)
        foot[span] = jnp.maximum(
            base.astype(F32) + (delta[span] - coupling) / scale, 0.0
        ).astype(BF16)
        store = pltpu.make_async_copy(foot.at[span], foot_hbm.at[span], sems.at[1 + n])
        store.start()
        stores.append(store)
    for store in stores:
        store.wait()


def solution(mesh):
    slabs, parts = mesh.shape["slab"], mesh.shape["tm"]

    def on_device(recording, footprints, traces, live_count):
        frames, voxels = recording.shape
        rows, neurons = footprints.shape
        rim = rows - voxels
        share = rows // parts
        half = parts // 2
        dims = (slabs, parts, frames, voxels, rows, neurons)
        hbm = pl.BlockSpec(memory_space=pltpu.HBM)
        vmem = pl.BlockSpec(memory_space=pltpu.VMEM)
        packed = share // 128 * frames + share % 128 // 2
        dma = pltpu.SemaphoreType.DMA
        tr, b_all, yt, side, mine, q_part, m_part = pl.pallas_call(
            functools.partial(exchange_kernel, dims),
            out_shape=[
                pltpu.VMEM((frames, neurons), F32),
                pltpu.VMEM((parts, frames, neurons), BF16),
                pltpu.VMEM((share, half * frames), BF16),
                pltpu.VMEM((parts, frames, rim), BF16),
                pltpu.VMEM((share, neurons), BF16),
                pltpu.VMEM((neurons, neurons), F32),
                pltpu.VMEM((share, neurons), F32),
            ],
            in_specs=[hbm, hbm, hbm, hbm],
            out_specs=[vmem] * 7,
            scratch_shapes=[
                pltpu.SMEM((slabs,), jnp.int32),
                pltpu.VMEM((frames, voxels), BF16),
                pltpu.VMEM((rows, neurons), BF16),
                pltpu.VMEM((frames, neurons), F32),
                pltpu.VMEM((parts, packed, 128), BF16),
                pltpu.VMEM((parts, packed, 128), BF16),
                pltpu.VMEM((frames, rim), BF16),
                pltpu.VMEM((frames, rim), F32),
                pltpu.VMEM((frames, rim), F32),
                pltpu.VMEM((frames, rim), F32),
                pltpu.VMEM((frames, rim), F32),
                pltpu.VMEM((half + 1, frames, rim), BF16),
                pltpu.VMEM((frames, rim), BF16),
                dma((6,)),
                dma((parts,)),
                dma((parts,)),
                dma((PIECES * parts,)),
                dma((PIECES * parts,)),
                dma((3,)),
                dma((3,)),
                dma((3,)),
                dma((parts + 1,)),
                pltpu.SemaphoreType.REGULAR,
                pltpu.SemaphoreType.REGULAR,
            ],
            compiler_params=pltpu.CompilerParams(
                collective_id=0, has_side_effects=True, vmem_limit_bytes=60 * 2**20
            ),
            name="exchange",
        )(live_count, recording, footprints, traces)
        return pl.pallas_call(
            functools.partial(update_kernel, dims),
            out_shape=[
                jax.ShapeDtypeStruct((frames, neurons), F32),
                jax.ShapeDtypeStruct((share, neurons), BF16),
            ],
            in_specs=[vmem] * 7,
            out_specs=[hbm, hbm],
            scratch_shapes=[
                pltpu.VMEM((share, neurons), BF16),
                dma((3,)),
            ],
            compiler_params=pltpu.CompilerParams(vmem_limit_bytes=32 * 2**20),
            name="update",
        )(tr, b_all, yt, side, mine, q_part, m_part)

    placed = (P("tm", "slab"), P(None, "slab"), P("tm", "slab"), P())
    return jax.shard_map(
        on_device,
        mesh=mesh,
        in_specs=placed,
        out_specs=(P("tm", "slab"), P("tm", "slab")),
        check_vma=False,
    )
```
